256 devices in a mesh: dp: 32 (over y, x, z_hi), section: 4 (over z_lo), tensor: 2 (over core).
Axes of the slice: x: 4, y: 4, z: 8 (z_hi: 2, z_lo: 4; z = z_hi * 4 + z_lo), core: 2. Of those that a mesh axis runs over, the one named last changes fastest.
Arguments:
- tokens_in: bfloat16 [4096, 3584], P('dp', 'tensor'), may hold values from -8 to 8
- query_gain: float32 [4, 3584], P('section', 'tensor'), may hold values from -1.5 to 1.5
- key_gain: float32 [4, 3584], P('section', 'tensor'), may hold values from -1.5 to 1.5
- value_gain: float32 [4, 3584], P('section', 'tensor'), may hold values from 0.5 to 2
- out_weight: bfloat16 [4, 3584, 3584], P('section', 'tensor', 'dp'), may hold values from -0.1875 to 0.1875
- doc_lengths: int32 [32, 4], P('dp'), may hold values from 1 to 64, 128 in all within a row
- grad_out: bfloat16 [4096, 3584], P('dp', 'tensor'), may hold values from -6 to 6
Outputs:
- layer_outputs: bfloat16 [4, 4096, 3584], P('section', 'dp', 'tensor')
- input_grads: bfloat16 [4, 4096, 3584], P('section', 'dp', 'tensor')
- weight_grads: float32 [4, 3584, 3584], P('section', 'tensor', 'dp')
The draws below stay inside these ranges and needn't reach their ends.
Inputs may be any that keep to these rules, and one draw needn't show every extreme that they name: `doc_lengths`: each row sums to 128; the longest document of every row has exactly 64 tokens.
All inputs are finite; a program needn't handle non-finite values.
Results may differ from the reference program's by a relative error of at most 0.035.
Values may be sent and summed in bfloat16 or wider, within the bound.
No kernel may reach another device: no remote copies, remote signals or barrier semaphores. Data moves between devices by JAX's collectives and lax.ppermute only.
A program may use at most 128 MiB of HBM per device.

```python
import math
import jax
import jax.numpy as jnp
import numpy as np
from jax import lax

HEADS = 28
HEAD_DIM = 128
D = 3584
SEQ = 128
DOCS = 4
LAYERS = 4
BATCH = 32
N_TENSOR = 2


PAIR_STEP = 0.015


def drawn_head(key):
    return jax.random.randint(jax.random.fold_in(key, 101), (), 0, HEADS)


def draw_tokens_in(key, part):
    head = drawn_head(key)
    key = jax.random.fold_in(key, 11)
    streams = jax.random.split(key, 6)
    count = BATCH * SEQ
    noise = jnp.clip(jax.random.normal(streams[2], (count, D), jnp.float32), -6.0, 6.0)
    signs = jnp.where(jax.random.bernoulli(streams[3], 0.5, (count, D)), 1.0, -1.0).astype(jnp.float32)
    base = signs * jax.random.uniform(streams[4], (count, D), jnp.float32, 0.6, 0.985)
    starts = jax.random.randint(streams[5], (BATCH, 3), 0, SEQ - 1)
    places = jnp.arange(count, dtype=jnp.int32)
    row_starts = starts[places // SEQ]
    firsts = (places % SEQ)[:, None] == row_starts
    strength = jnp.array([7.8, 7.0, 6.0], dtype=jnp.float32)
    quiet = jnp.array([0.15, 0.3, 0.5], dtype=jnp.float32)
    amp_first = jnp.max(jnp.where(firsts, strength[None, :], 0.0), axis=1)
    damp_first = jnp.min(jnp.where(firsts, quiet[None, :], 1.0), axis=1)
    is_first = jnp.any(firsts, axis=1)
    is_second = jnp.roll(is_first, 1)
    amp = jnp.where(is_second, jnp.roll(amp_first, 1), amp_first)
    damp = jnp.where(is_second, jnp.roll(damp_first, 1), damp_first)
    shifted_base = jnp.roll(base, 1, axis=0)
    shifted_noise = jnp.roll(noise, 1, axis=0)
    feature = jnp.arange(D, dtype=jnp.int32)
    in_head = feature // HEAD_DIM == head
    even = feature % 2 == 0
    first_head = jnp.where(even[None, :], base, 0.5 * base) * amp[:, None]
    second_head = jnp.where(even[None, :], (1.0 + PAIR_STEP) * shifted_base, -0.5 * shifted_base) * amp[:, None]
    head_part = jnp.where(is_second[:, None], second_head, first_head)
    other_part = jnp.where(is_second[:, None], shifted_noise, noise) * damp[:, None]
    planted = jnp.where(in_head[None, :], head_part, other_part)
    chosen = is_first | is_second
    return jnp.where(chosen[:, None], planted, noise).astype(jnp.bfloat16)


def draw_query_gain(key, part):
    head = drawn_head(key)
    key = jax.random.fold_in(key, 12)
    first_key, second_key = jax.random.split(key)
    spread = jax.random.uniform(first_key, (LAYERS, D), jnp.float32, -1.5, 1.5)
    strong = jax.random.uniform(second_key, (LAYERS, D), jnp.float32, 1.2, 1.5)
    in_head = jnp.arange(D, dtype=jnp.int32) // HEAD_DIM == head
    return jnp.where(in_head[None, :], strong, spread)


def draw_key_gain(key, part):
    head = drawn_head(key)
    key = jax.random.fold_in(key, 13)
    first_key, second_key, third_key = jax.random.split(key, 3)
    spread = jax.random.uniform(first_key, (LAYERS, D), jnp.float32, -1.5, 1.5)
    strong = jax.random.uniform(second_key, (LAYERS, D), jnp.float32, 1.2, 1.5)
    faint = jax.random.uniform(third_key, (LAYERS, D), jnp.float32, 0.005, 0.01)
    feature = jnp.arange(D, dtype=jnp.int32)
    in_head = feature // HEAD_DIM == head
    even = feature % 2 == 0
    inside = jnp.where(even[None, :], strong, faint)
    return jnp.where(in_head[None, :], inside, spread)


def raised(entries, key, source, target, shards_of, factor):
    def block_of(dim):
        return (jnp.arange(entries.shape[dim]) // (entries.shape[dim] // shards_of)).reshape((-1,) + (1,) * (entries.ndim - 1 - dim))

    one_side = jax.random.permutation(key, shards_of)[block_of(target)]
    far = (block_of(target) + shards_of // 2) % shards_of
    return jnp.where((block_of(source) == one_side) | (block_of(source) == far), factor * entries, entries)


def block_scale(rng, dims, cuts, low, largest):
    def one(position, shards_of):
        heights = jax.random.uniform(jax.random.fold_in(jax.random.fold_in(rng, 6), position), (shards_of,), jnp.float32, low / len(cuts), largest / len(cuts))
        return jnp.repeat(jnp.exp(heights), dims[position] // shards_of).reshape((-1,) + (1,) * (len(dims) - position - 1))

    gain = one(*cuts[0])
    for cut in cuts[1:]:
        gain = gain * one(*cut)
    return gain


def length_profile(number_of, total, bound, lean):
    loads = [(1 << 20) // math.isqrt(standing ** lean) + 1 for standing in range(2, number_of + 1)]
    spare, holding = total - bound - (number_of - 1), [1] * (number_of - 1)
    while spare > 0:
        free = [i for i in range(number_of - 1) if holding[i] < bound]
        pool, left = sum([loads[i] for i in free]), spare
        for i in free:
            more = min(bound - holding[i], max(1, left * loads[i] // pool), spare)
            holding[i] = holding[i] + more
            spare = spare - more
    return np.array([bound] + holding)


def uneven(stream_key, amount, total, bound, skew):
    if amount == 2:
        one = jax.random.randint(stream_key, (), max(1, total - bound), min(bound, total - 1) + 1)
        return jnp.stack([one, total - one])
    sizes = jnp.asarray(length_profile(amount, total, bound, skew), jnp.int32)
    pairs = (amount - 1) // 2
    source_of, receiver = sizes[1:1 + 2 * pairs:2], sizes[2:2 + 2 * pairs:2]
    room = jnp.minimum(source_of - 1, bound - receiver)
    moved = jax.random.randint(jax.random.fold_in(stream_key, 1), (pairs,), 0, 1 << 20) % (room + 1)
    sizes = sizes.at[1:1 + 2 * pairs:2].set(source_of - moved).at[2:2 + 2 * pairs:2].set(receiver + moved)
    return sizes[jax.random.permutation(jax.random.fold_in(stream_key, 2), amount)]


def bell_draw(rng, dims, scale, most, pieces=(), kind=jnp.bfloat16):
    level = block_scale(rng, dims, pieces, -0.22, 0.18) if pieces else 1.0
    drawn = jax.random.normal(rng, dims, jnp.float32) * scale * level
    return jnp.minimum(jnp.maximum(drawn, -most), most).astype(kind)


def bell_draw_with(stream_key, dims, deviation, reach, cuts, heavy, held_as=jnp.bfloat16):
    entries = deviation * jax.random.normal(stream_key, dims, jnp.float32)
    if cuts:
        entries = entries * block_scale(stream_key, dims, cuts, -0.22, 0.18)
    return jnp.clip(raised(entries, jax.random.fold_in(stream_key, 3), *heavy), -reach, reach).astype(held_as)


def setup_inputs(seed: int = 0) -> dict:
    streams_of = jax.random.split(jax.random.key(seed), 8)
    tokens_in = draw_tokens_in(jax.random.fold_in(streams_of[7], 71), 0)
    query_gain = draw_query_gain(jax.random.fold_in(streams_of[7], 71), 0)
    key_gain = draw_key_gain(jax.random.fold_in(streams_of[7], 71), 0)
    value_gain = jnp.clip(jnp.exp(math.log(2.0) - 1.3862944 * jax.random.uniform(streams_of[3], (LAYERS, D), jnp.float32) ** block_scale(streams_of[3], (LAYERS, D), ((0, 4), (1, 2)), -0.2, 0.2)), 0.5, 2.0)
    out_weight = bell_draw(streams_of[4], (LAYERS, D, D), (D // 4) ** -0.5, 0.1875, ((0, 4), (1, 2), (2, 32)))
    doc_lengths = jax.vmap(lambda own: uneven(own, DOCS, SEQ, SEQ // 2, 2))(jax.random.split(streams_of[5], BATCH)).reshape((BATCH, DOCS)).astype(jnp.int32)
    grad_out = bell_draw_with(streams_of[6], (BATCH * SEQ, D), 1.0, 6.0, ((0, 32), (1, 2)), (0, 1, 32, 2.75))
    return {"tokens_in": tokens_in, "query_gain": query_gain, "key_gain": key_gain, "value_gain": value_gain, "out_weight": out_weight, "doc_lengths": doc_lengths, "grad_out": grad_out}


EPS = 1e-05

def doc_mask(lengths, count):
    ends = jnp.cumsum(lengths.astype(jnp.int32))
    places = jnp.arange(count, dtype=jnp.int32)
    ident = lax.optimization_barrier(jnp.sum((places[:, None] >= ends[None, :]).astype(jnp.int32), axis=1))
    causal = places[None, :] <= places[:, None]
    return causal & (ident[:, None] == ident[None, :])

def attend_exact(query_src, key_src, gains, allowed):
    rows_q = query_src.shape[0]
    rows_k = key_src.shape[0]
    queries = (query_src * gains[0]).reshape(rows_q, -1, HEAD_DIM)
    keys = (key_src * gains[1]).reshape(rows_k, -1, HEAD_DIM)
    values = (key_src * gains[2]).reshape(rows_k, -1, HEAD_DIM)
    scores = jnp.einsum('qhd,khd->hqk', queries, keys, precision=lax.Precision.HIGHEST) / jnp.sqrt(jnp.float32(HEAD_DIM))
    scores = jnp.where(allowed[None], scores, -1e+30)
    top = lax.stop_gradient(lax.optimization_barrier(jnp.max(scores, axis=-1, keepdims=True)))
    expo = jnp.exp(scores - top)
    probs = expo / lax.optimization_barrier(jnp.sum(expo, axis=-1, keepdims=True))
    mixed = jnp.einsum('hqk,khd->qhd', probs, values, precision=lax.Precision.HIGHEST)
    return mixed.reshape(rows_q, -1)

def attend_rounded(normed, gains, allowed):
    rows = normed.shape[0]
    queries = (normed * gains[0]).astype(jnp.bfloat16).astype(jnp.float32).reshape(rows, -1, HEAD_DIM)
    keys = (normed * gains[1]).astype(jnp.bfloat16).astype(jnp.float32).reshape(rows, -1, HEAD_DIM)
    values = (normed * gains[2]).astype(jnp.bfloat16).astype(jnp.float32).reshape(rows, -1, HEAD_DIM)
    scores = jnp.einsum('qhd,khd->hqk', queries, keys, precision=lax.Precision.HIGHEST) / jnp.sqrt(jnp.float32(HEAD_DIM))
    scores = jnp.where(allowed[None], scores, -1e+30)
    top = lax.optimization_barrier(jnp.max(scores, axis=-1, keepdims=True))
    expo = jnp.exp(scores - top)
    probs = (expo / lax.optimization_barrier(jnp.sum(expo, axis=-1, keepdims=True))).astype(jnp.bfloat16).astype(jnp.float32)
    mixed = jnp.einsum('hqk,khd->qhd', probs, values, precision=lax.Precision.HIGHEST)
    return mixed.reshape(rows, -1).astype(jnp.bfloat16)

def one_sequence(seq_tokens, seq_lengths, seq_grads, query_gain, key_gain, value_gain, out_weight):
    allowed = doc_mask(seq_lengths, SEQ)
    half = D // N_TENSOR
    current = seq_tokens
    saved = []
    outputs = []
    for layer in range(LAYERS):
        gains = (query_gain[layer], key_gain[layer], value_gain[layer])
        inputs_f = current.astype(jnp.float32)
        inverse = lax.rsqrt(lax.optimization_barrier(jnp.mean(inputs_f * inputs_f, axis=1)) + EPS)
        normed = inputs_f * inverse[:, None]
        mixed = attend_rounded(normed, gains, allowed)
        summed = jnp.zeros((SEQ, D), jnp.float32)
        for part in range(N_TENSOR):
            piece = jnp.dot(mixed[:, part * half:(part + 1) * half], out_weight[layer, part * half:(part + 1) * half], preferred_element_type=jnp.float32)
            summed = summed + lax.optimization_barrier(piece.astype(jnp.bfloat16)).astype(jnp.float32)
        current = (inputs_f + summed).astype(jnp.bfloat16)
        saved.append((inputs_f, inverse, mixed, gains))
        outputs.append(current)
    grad_now = seq_grads
    input_grads = [None] * LAYERS
    terms = [None] * LAYERS
    for layer in range(LAYERS - 1, -1, -1):
        inputs_f, inverse, mixed, gains = saved[layer]
        grad_mixed = jnp.dot(grad_now, out_weight[layer].T, preferred_element_type=jnp.float32)
        term = jnp.dot(mixed.T, grad_now, preferred_element_type=jnp.float32)
        terms[layer] = lax.optimization_barrier(term.astype(jnp.bfloat16)).astype(jnp.float32)
        normed = inputs_f * inverse[:, None]
        _, pull = jax.vjp(lambda query_src, key_src: attend_exact(query_src, key_src, gains, allowed), normed, normed)
        grad_query, grad_key = pull(grad_mixed)
        grad_normed = grad_query + grad_key
        grad_inverse = lax.optimization_barrier(jnp.sum(grad_normed * inputs_f, axis=1))
        grad_in = grad_now.astype(jnp.float32) + grad_normed * inverse[:, None] - inputs_f * (grad_inverse * inverse * inverse * inverse / D)[:, None]
        grad_now = grad_in.astype(jnp.bfloat16)
        input_grads[layer] = grad_now
    return (jnp.stack(outputs), jnp.stack(input_grads), jnp.stack(terms))

def reference(tokens_in, query_gain, key_gain, value_gain, out_weight, doc_lengths, grad_out):
    seqs_in = tokens_in.reshape(BATCH, SEQ, D)
    grads_in = grad_out.reshape(BATCH, SEQ, D)

    def advance(total, items):
        seq_tokens, seq_lengths, seq_grads = items
        outs, grads, terms = one_sequence(seq_tokens, seq_lengths, seq_grads, query_gain, key_gain, value_gain, out_weight)
        return (total + terms, (outs, grads))
    total, (outs, grads) = lax.scan(advance, jnp.zeros((LAYERS, D, D), jnp.float32), (seqs_in, doc_lengths, grads_in))
    layer_outputs = jnp.transpose(outs, (1, 0, 2, 3)).reshape(LAYERS, BATCH * SEQ, D)
    input_grads = jnp.transpose(grads, (1, 0, 2, 3)).reshape(LAYERS, BATCH * SEQ, D)
    return (layer_outputs, input_grads, total)
```

```python
import jax
import jax.numpy as jnp
from jax import lax
from jax.experimental import pallas as pl
from jax.experimental.pallas import tpu as pltpu
from jax.sharding import PartitionSpec as P

HEAD_DIM = 128
EPS = 1e-05
CHUNK = 256
F32 = jnp.float32
BF16 = jnp.bfloat16
NN = (((1,), (0,)), ((), ()))
NT = (((1,), (1,)), ((), ()))
TN = (((0,), (0,)), ((), ()))
VMEM_LIMIT = 48 * 1024 * 1024


def dot(a, b, dims):
    return lax.dot_general(a, b, dims, preferred_element_type=F32)


def split(a):
    high = a.astype(BF16)
    return high, (a - high.astype(F32)).astype(BF16)


def weight_copies(half, weight_ref, held, sems):
    rows, width = held.shape
    copies = []
    for i in range(rows // CHUNK):
        source = lax.rem(half * width + i * CHUNK, rows)
        source = pl.multiple_of(source, CHUNK)
        copies.append(
            pltpu.make_async_copy(
                weight_ref.at[pl.ds(source, CHUNK)], held.at[pl.ds(i * CHUNK, CHUNK)], sems.at[i]
            )
        )
    return copies


def allowed_mask(id_col, id_row):
    shape = (id_col.shape[0], id_row.shape[1])
    rows = lax.broadcasted_iota(jnp.int32, shape, 0)
    cols = lax.broadcasted_iota(jnp.int32, shape, 1)
    return (rows >= cols) & (id_col[...] == id_row[...])


def forward_kernel(
    half_ref, x_ref, squares_ref, gq_ref, gk_ref, gv_ref, id_col, id_row, weight_ref,
    own_ref, other_ref, mixed_ref, held, sems,
):
    copies = weight_copies(half_ref[0], weight_ref, held, sems)
    for copy in copies:
        copy.start()
    width = x_ref.shape[1]
    inverse = lax.rsqrt(squares_ref[...] / (2 * width) + EPS)
    allowed = allowed_mask(id_col, id_row)
    scale = HEAD_DIM**-0.5
    for head in range(width // HEAD_DIM):
        cols = slice(head * HEAD_DIM, (head + 1) * HEAD_DIM)
        normed = x_ref[:, cols].astype(F32) * inverse
        queries = (normed * gq_ref[:, cols]).astype(BF16)
        keys = (normed * gk_ref[:, cols]).astype(BF16)
        values = (normed * gv_ref[:, cols]).astype(BF16)
        scores = jnp.where(allowed, dot(queries, keys, NT) * scale, -1e30)
        expo = jnp.exp(scores - jnp.max(scores, axis=1, keepdims=True))
        probs = (expo / jnp.sum(expo, axis=1, keepdims=True)).astype(BF16)
        mixed_ref[:, cols] = dot(probs, values, NN).astype(BF16)
    mixed = mixed_ref[...]
    per_half = width // CHUNK
    for i, copy in enumerate(copies):
        copy.wait()
        piece = dot(mixed, held[i * CHUNK : (i + 1) * CHUNK], NT).astype(BF16)
        target = own_ref if i < per_half else other_ref
        start = (i % per_half) * CHUNK
        target[:, start : start + CHUNK] = piece


def backward_kernel(
    half_ref, x_ref, squares_ref, gq_ref, gk_ref, gv_ref, id_col, id_row, weight_ref,
    grad_ref, grad_other_ref, sum_ref, inner_ref, held, probs_buf, sems,
):
    copies = weight_copies(half_ref[0], weight_ref, held, sems)
    for copy in copies:
        copy.start()
    width = x_ref.shape[1]
    heads = width // HEAD_DIM
    inverse = lax.rsqrt(squares_ref[...] / (2 * width) + EPS)
    allowed = allowed_mask(id_col, id_row)
    scale = HEAD_DIM**-0.5
    for head in range(heads):
        cols = slice(head * HEAD_DIM, (head + 1) * HEAD_DIM)
        normed = x_ref[:, cols].astype(F32) * inverse
        q_high, q_low = split(normed * gq_ref[:, cols])
        k_high, k_low = split(normed * gk_ref[:, cols])
        scores = dot(
            jnp.concatenate([q_high, q_high, q_low], axis=1),
            jnp.concatenate([k_high, k_low, k_high], axis=1),
            NT,
        )
        scores = jnp.where(allowed, scores * scale, -1e30)
        expo = jnp.exp(scores - jnp.max(scores, axis=1, keepdims=True))
        probs_buf[head] = expo / jnp.sum(expo, axis=1, keepdims=True)
    for copy in copies:
        copy.wait()
    inner = jnp.zeros((x_ref.shape[0], HEAD_DIM), F32)
    for pair in range(width // CHUNK):
        wide = slice(pair * CHUNK, (pair + 1) * CHUNK)
        grad_mixed = dot(grad_ref[...], held[:width, wide], NN) + dot(
            grad_other_ref[...], held[width:, wide], NN
        )
        for part in range(CHUNK // HEAD_DIM):
            head = pair * (CHUNK // HEAD_DIM) + part
            cols = slice(head * HEAD_DIM, (head + 1) * HEAD_DIM)
            grad_head = grad_mixed[:, part * HEAD_DIM : (part + 1) * HEAD_DIM].astype(BF16)
            x_head = x_ref[:, cols].astype(F32)
            normed = x_head * inverse
            queries = (normed * gq_ref[:, cols]).astype(BF16)
            keys = (normed * gk_ref[:, cols]).astype(BF16)
            values = (normed * gv_ref[:, cols]).astype(BF16)
            probs = probs_buf[head]
            grad_values = dot(probs.astype(BF16), grad_head, TN)
            weighted = probs * dot(grad_head, values, NT)
            grad_scores = weighted - probs * jnp.sum(weighted, axis=1, keepdims=True)
            grad_scores = (grad_scores * scale).astype(BF16)
            grad_queries = dot(grad_scores, keys, NN)
            grad_keys = dot(grad_scores, queries, TN)
            grad_normed = (
                grad_queries * gq_ref[:, cols]
                + grad_keys * gk_ref[:, cols]
                + grad_values * gv_ref[:, cols]
            )
            inner = inner + grad_normed * x_head
            sum_ref[:, cols] = grad_ref[:, cols].astype(F32) + grad_normed * inverse
    inner_ref[...] = jnp.sum(inner, axis=1, keepdims=True)


VMEM = pl.BlockSpec(memory_space=pltpu.VMEM)
SMEM = pl.BlockSpec(memory_space=pltpu.SMEM)
ANY = pl.BlockSpec(memory_space=pl.ANY)


def forward_call(rows, width):
    full = 2 * width
    shape = jax.ShapeDtypeStruct((rows, width), BF16)
    return pl.pallas_call(
        forward_kernel,
        out_shape=(shape, shape, shape),
        in_specs=[SMEM] + [VMEM] * 7 + [ANY],
        out_specs=(VMEM, VMEM, VMEM),
        scratch_shapes=[
            pltpu.VMEM((full, width), BF16),
            pltpu.SemaphoreType.DMA((full // CHUNK,)),
        ],
        compiler_params=pltpu.CompilerParams(vmem_limit_bytes=VMEM_LIMIT),
        name="layer_forward",
    )


def backward_call(rows, width):
    full = 2 * width
    return pl.pallas_call(
        backward_kernel,
        out_shape=(
            jax.ShapeDtypeStruct((rows, width), F32),
            jax.ShapeDtypeStruct((rows, 1), F32),
        ),
        in_specs=[SMEM] + [VMEM] * 7 + [ANY] + [VMEM] * 2,
        out_specs=(VMEM, VMEM),
        scratch_shapes=[
            pltpu.VMEM((full, width), BF16),
            pltpu.VMEM((width // HEAD_DIM, rows, rows), F32),
            pltpu.SemaphoreType.DMA((full // CHUNK,)),
        ],
        compiler_params=pltpu.CompilerParams(vmem_limit_bytes=VMEM_LIMIT),
        name="layer_backward",
    )


def local(tokens_in, query_gain, key_gain, value_gain, out_weight, doc_lengths, grad_out):
    rows, width = tokens_in.shape
    full = 2 * width
    sections = lax.axis_size("section")
    shards = lax.axis_size("dp")
    section = lax.axis_index("section")
    half = lax.axis_index("tensor").astype(jnp.int32).reshape(1)

    def swap(block):
        return lax.ppermute(block, "tensor", [(0, 1), (1, 0)])

    def relay(block, step):
        route = [(i, i + step) for i in range(sections) if 0 <= i + step < sections]
        return lax.ppermute(block, "section", route)

    ends = jnp.cumsum(doc_lengths[0])
    ident = jnp.sum(
        (jnp.arange(rows, dtype=jnp.int32)[:, None] >= ends[None, :]).astype(jnp.int32), axis=1
    )
    id_col, id_row = ident[:, None], ident[None, :]
    gains = (query_gain, key_gain, value_gain)
    weight = lax.all_gather(out_weight[0].T, "dp", axis=0, tiled=True)

    def row_squares(block):
        wide = block.astype(F32)
        own = jnp.sum(wide * wide, axis=1, keepdims=True)
        return own + swap(own)

    first_squares = row_squares(tokens_in)
    forward = forward_call(rows, width)
    x, squares = tokens_in, first_squares
    for turn in range(sections):
        own, other, mixed = forward(half, x, squares, *gains, id_col, id_row, weight)
        total = own.astype(F32) + swap(other).astype(F32)
        output = (x.astype(F32) + total).astype(BF16)
        if turn < sections - 1:
            arrived = relay(output, 1)
            arrived_squares = relay(row_squares(output), 1)
            x = jnp.where(section == 0, tokens_in, arrived)
            squares = jnp.where(section == 0, first_squares, arrived_squares)

    mixed_all = lax.all_gather(mixed, "dp", axis=0)

    backward = backward_call(rows, width)
    inverse = lax.rsqrt(squares / full + EPS)
    x_wide = x.astype(F32)
    grad = grad_out
    for turn in range(sections):
        grad_other = swap(grad)
        pulled, inner = backward(
            half, x, squares, *gains, id_col, id_row, weight, grad, grad_other
        )
        inner = inner + swap(inner)
        grad_in = (pulled - x_wide * (inner * inverse * inverse * inverse / full)).astype(BF16)
        if turn < sections - 1:
            arrived = relay(grad_in, -1)
            grad = jnp.where(section == sections - 1, grad_out, arrived)

    first = jnp.where(half[0] == 0, grad, grad_other)
    second = jnp.where(half[0] == 0, grad_other, grad)
    columns = jnp.concatenate([first.T, second.T], axis=0).reshape(shards, full // shards, rows)
    columns = lax.all_to_all(columns, "dp", split_axis=0, concat_axis=0)
    weight_grads = lax.dot_general(
        mixed_all, columns, (((0, 1), (0, 2)), ((), ())), preferred_element_type=F32
    )
    return output[None], grad_in[None], weight_grads[None]


def solution(mesh):
    return jax.shard_map(
        local,
        mesh=mesh,
        in_specs=(
            P("dp", "tensor"),
            P("section", "tensor"),
            P("section", "tensor"),
            P("section", "tensor"),
            P("section", "tensor", "dp"),
            P("dp", None),
            P("dp", "tensor"),
        ),
        out_specs=(
            P("section", "dp", "tensor"),
            P("section", "dp", "tensor"),
            P("section", "tensor", "dp"),
        ),
        check_vma=False,
    )
```

```python
import jax
import jax.numpy as jnp
from jax import lax
from jax.experimental import pallas as pl
from jax.experimental.pallas import tpu as pltpu
from jax.sharding import PartitionSpec as P

HEAD_DIM = 128
EPS = 1e-05
CHUNK = 256
SIDE = 4
LAYERS_DEEP = 2
F32 = jnp.float32
BF16 = jnp.bfloat16
NN = (((1,), (0,)), ((), ()))
NT = (((1,), (1,)), ((), ()))
TN = (((0,), (0,)), ((), ()))
VMEM_LIMIT = 56 * 1024 * 1024
FIRST_OFFSETS = (0, -1, -2, 1)


def dot(a, b, dims):
    return lax.dot_general(a, b, dims, preferred_element_type=F32)


def split(a):
    high = a.astype(BF16)
    return high, (a - high.astype(F32)).astype(BF16)


def grid_index(y, x, plane):
    return ((y % SIDE) * SIDE + x % SIDE) * LAYERS_DEEP + plane % LAYERS_DEEP


def shift(block, axis, step):
    move = {"y": (step, 0, 0), "x": (0, step, 0), "plane": (0, 0, step)}[axis]
    route = [
        (grid_index(y, x, p), grid_index(y + move[0], x + move[1], p + move[2]))
        for y in range(SIDE)
        for x in range(SIDE)
        for p in range(LAYERS_DEEP)
    ]
    return lax.ppermute(block, "dp", route)


def tied(blocks, *others):
    return list(lax.optimization_barrier(tuple(blocks) + tuple(others))[: len(blocks)])


def gather_weight(shard):
    width = shard.shape[1] // 2
    sides = ((slice(0, width), "x", "y"), (slice(width, 2 * width), "y", "x"))
    seconds = [side[2] for side in sides]

    def first_ring(block):
        joined = []
        for cols, axis, _ in sides:
            own = block[:, cols]
            back, ahead = shift(own, axis, 1), shift(own, axis, -1)
            joined.append(jnp.concatenate([own, back, shift(back, axis, 1), ahead], axis=0))
        return joined

    def both(blocks, step):
        return [shift(block, axis, step) for block, axis in zip(blocks, seconds)]

    far_shard = shift(shard, "plane", 1)
    near = tied(first_ring(shard))
    near_back, near_ahead = both(near, 1), both(near, -1)
    far = first_ring(far_shard)
    near_back = tied(near_back)
    near_across = both(near_back, 1)
    far = tied(far, *near_back, *near_ahead)
    far_ahead = both(far, -1)
    late = tied(far, *near_across)
    far_back = both(late, 1)
    far_across = both(far_ahead, -1)
    pieces = []
    for side in range(2):
        for plane, group in enumerate(
            ((near, near_back, near_ahead, near_across), (far, far_back, far_ahead, far_across))
        ):
            for offset, blocks in zip((0, -1, 1, -2), group):
                pieces.append((side, plane, offset, blocks[side]))
    return pieces


def exchange_columns(grad_t, y, x, half):
    shards = grad_t.reshape(2, SIDE, -1, grad_t.shape[1])
    got = []
    for step in range(SIDE):
        part = lax.dynamic_index_in_dim(shards, (x + step) % SIDE, 1, keepdims=False)
        got.append(shift(part, "x", step) if step else part)
    got = jnp.stack(got, axis=1)
    result = []
    for step in range(SIDE):
        part = lax.dynamic_index_in_dim(got, (y + step) % 2, 0, keepdims=False)
        if step:
            route = []
            for row in range(SIDE):
                target = (row + step) % SIDE
                for col in range(SIDE):
                    for p in range(LAYERS_DEEP):
                        source, sink = grid_index(row, col, p), grid_index(target, col, p)
                        route.append((source * 2 + target // 2, sink * 2 + target // 2))
            part = lax.ppermute(part, ("dp", "tensor"), route)
        result.append(part)
    result = jnp.stack(result)
    return jnp.where(y // 2 == half, result, swap(result))


def swap(block):
    return lax.ppermute(block, "tensor", [(0, 1), (1, 0)])


def relay(block, step):
    sections = lax.axis_size("section")
    route = [(i, i + step) for i in range(sections) if 0 <= i + step < sections]
    return lax.ppermute(block, "section", route)


def allowed_mask(id_col, id_row):
    shape = (id_col.shape[0], id_row.shape[1])
    rows = lax.broadcasted_iota(jnp.int32, shape, 0)
    cols = lax.broadcasted_iota(jnp.int32, shape, 1)
    return (rows >= cols) & (id_col[...] == id_row[...])


def softmax(scores, allowed):
    scores = jnp.where(allowed, scores * HEAD_DIM**-0.5, -1e30)
    expo = jnp.exp(scores - jnp.max(scores, axis=1, keepdims=True))
    return expo / jnp.sum(expo, axis=1, keepdims=True)


def head_slices(width):
    return [slice(i, i + HEAD_DIM) for i in range(0, width, HEAD_DIM)]


def attend(x_ref, squares_ref, gq_ref, gk_ref, gv_ref, id_col, id_row, probs_buf, values_buf, mixed_ref):
    width = x_ref.shape[1]
    inverse = lax.rsqrt(squares_ref[...] / (2 * width) + EPS)
    allowed = allowed_mask(id_col, id_row)
    for head, cols in enumerate(head_slices(width)):
        normed = x_ref[:, cols].astype(F32) * inverse
        queries = (normed * gq_ref[:, cols]).astype(BF16)
        keys = (normed * gk_ref[:, cols]).astype(BF16)
        values_buf[:, cols] = (normed * gv_ref[:, cols]).astype(BF16)
        probs_buf[head] = softmax(dot(queries, keys, NT), allowed).astype(BF16)
    for head, cols in enumerate(head_slices(width)):
        mixed_ref[:, cols] = dot(probs_buf[head], values_buf[:, cols], NN).astype(BF16)


def start_all(copies):
    for copy in copies:
        copy.start()


def project(piece, index, own_ref, other_ref):
    per_half = own_ref.shape[1] // CHUNK
    target = own_ref if index < per_half else other_ref
    start = (index % per_half) * CHUNK
    target[:, start : start + CHUNK] = piece.astype(BF16)


def first_kernel(layout, place_ref, *refs):
    inputs, refs = refs[:7], refs[7:]
    pieces, refs = refs[: len(layout)], refs[len(layout) :]
    own_ref, other_ref, rows_out, cols_out = refs[:4]
    mixed_ref, probs_buf, values_buf, held, turned, in_sems, out_sems = refs[4:]
    y, x, plane, half = [place_ref[i] for i in range(4)]
    full, width = held.shape
    shard = pieces[0].shape[0] // SIDE
    copies = []
    for (side, far, offset), piece in zip(layout, pieces):
        for part, first in enumerate(FIRST_OFFSETS):
            at_y, at_x = (offset, first) if side == 0 else (first, offset)
            row = lax.rem(y + at_y + SIDE, SIDE)
            col = lax.rem(x + at_x + SIDE, SIDE)
            depth = 1 - plane if far else plane
            index = (row * SIDE + col) * LAYERS_DEEP + depth
            start = lax.rem(index * shard + half * width, full)
            start = pl.multiple_of(start, 16)
            copies.append(
                pltpu.make_async_copy(
                    piece.at[pl.ds(part * shard, shard)],
                    held.at[pl.ds(start, shard), pl.ds(side * (width // 2), width // 2)],
                    in_sems.at[len(copies)],
                )
            )
    start_all(copies)
    attend(*inputs, probs_buf, values_buf, mixed_ref)
    for copy in copies:
        copy.wait()
    out = pltpu.make_async_copy(held, rows_out, out_sems.at[0])
    out.start()
    outs = [out]
    mixed = mixed_ref[...]
    for i in range(full // CHUNK):
        turned[i] = held[i * CHUNK : (i + 1) * CHUNK].T
        out = pltpu.make_async_copy(turned.at[i], cols_out.at[i], out_sems.at[1 + i])
        out.start()
        outs.append(out)
        project(dot(mixed, turned[i], NN), i, own_ref, other_ref)
    for out in outs:
        out.wait()


def forward_kernel(*refs):
    inputs, refs = refs[:7], refs[7:]
    weight_ref, own_ref, other_ref, mixed_ref, probs_buf, values_buf, held, sems = refs
    count = held.shape[0]
    copies = [
        pltpu.make_async_copy(weight_ref.at[i], held.at[i], sems.at[i]) for i in range(count)
    ]
    start_all(copies)
    attend(*inputs, probs_buf, values_buf, mixed_ref)
    mixed = mixed_ref[...]
    for i, copy in enumerate(copies):
        copy.wait()
        project(dot(mixed, held[i], NN), i, own_ref, other_ref)


def backward_kernel(
    x_ref, squares_ref, gq_ref, gk_ref, gv_ref, id_col, id_row, weight_ref, grad_ref,
    grad_other_ref, sum_ref, inner_ref, held, probs_buf, scores_buf, q_buf, k_buf, v_buf,
    mixed_buf, sems,
):
    full, width = held.shape
    copies = []
    for i in range(full // CHUNK):
        rows = pl.ds(i * CHUNK, CHUNK)
        copies.append(pltpu.make_async_copy(weight_ref.at[rows], held.at[rows], sems.at[i]))
    start_all(copies)
    inverse = lax.rsqrt(squares_ref[...] / full + EPS)
    allowed = allowed_mask(id_col, id_row)
    heads = head_slices(width)
    for head, cols in enumerate(heads):
        normed = x_ref[:, cols].astype(F32) * inverse
        q_high, q_low = split(normed * gq_ref[:, cols])
        k_high, k_low = split(normed * gk_ref[:, cols])
        q_buf[:, cols] = q_high
        k_buf[:, cols] = k_high
        v_buf[:, cols] = (normed * gv_ref[:, cols]).astype(BF16)
        scores = dot(
            jnp.concatenate([q_high, q_high, q_low], axis=1),
            jnp.concatenate([k_high, k_low, k_high], axis=1),
            NT,
        )
        probs_buf[head] = softmax(scores, allowed)
    per_half = width // CHUNK
    for i, copy in enumerate(copies):
        copy.wait()
        source = grad_ref if i < per_half else grad_other_ref
        start = (i % per_half) * CHUNK
        part = dot(source[:, start : start + CHUNK], held[i * CHUNK : (i + 1) * CHUNK], NN)
        mixed_buf[...] = part if i == 0 else mixed_buf[...] + part
    for head, cols in enumerate(heads):
        probs = probs_buf[head]
        weighted = probs * dot(mixed_buf[:, cols].astype(BF16), v_buf[:, cols], NT)
        inner = jnp.sum(weighted, axis=1, keepdims=True)
        scores_buf[head] = ((weighted - probs * inner) * HEAD_DIM**-0.5).astype(BF16)
    inner = jnp.zeros((x_ref.shape[0], HEAD_DIM), F32)
    for head, cols in enumerate(heads):
        grad_scores = scores_buf[head]
        grad_values = dot(probs_buf[head].astype(BF16), mixed_buf[:, cols].astype(BF16), TN)
        grad_normed = (
            dot(grad_scores, k_buf[:, cols], NN) * gq_ref[:, cols]
            + dot(grad_scores, q_buf[:, cols], TN) * gk_ref[:, cols]
            + grad_values * gv_ref[:, cols]
        )
        inner = inner + grad_normed * x_ref[:, cols].astype(F32)
        sum_ref[:, cols] = grad_ref[:, cols].astype(F32) + grad_normed * inverse
    inner_ref[...] = jnp.sum(inner, axis=1, keepdims=True)


def weight_kernel(place_ref, columns_ref, mixed_ref, own_ref, far_ref, held, total, sems):
    y, x, plane = [place_ref[i] for i in range(3)]
    count, shard_pair, rows = columns_ref.shape
    shard = shard_pair // LAYERS_DEEP
    copies = []
    for i in range(count):
        row = lax.rem(y - i // SIDE + SIDE, SIDE)
        col = lax.rem(x - i % SIDE + SIDE, SIDE)
        source = pl.multiple_of((row * SIDE + col) * rows, rows)
        copies.append(
            pltpu.make_async_copy(
                mixed_ref.at[pl.ds(source, rows)], held.at[pl.ds(i * rows, rows)], sems.at[i]
            )
        )
    start_all(copies)
    for i in range(0, count, SIDE):
        for copy in copies[i : i + SIDE]:
            copy.wait()
        left = jnp.concatenate([columns_ref[i + j] for j in range(SIDE)], axis=1)
        part = dot(left, held[i * rows : (i + SIDE) * rows], NN)
        total[...] = part if i == 0 else total[...] + part
    own_ref[...] = total[pl.ds(pl.multiple_of(plane * shard, 16), shard)]
    far_ref[...] = total[pl.ds(pl.multiple_of((1 - plane) * shard, 16), shard)].astype(BF16)


VMEM = pl.BlockSpec(memory_space=pltpu.VMEM)
SMEM = pl.BlockSpec(memory_space=pltpu.SMEM)
ANY = pl.BlockSpec(memory_space=pl.ANY)
PARAMS = pltpu.CompilerParams(vmem_limit_bytes=VMEM_LIMIT)


def attention_scratch(rows, width):
    heads = width // HEAD_DIM
    return [pltpu.VMEM((heads, rows, rows), BF16), pltpu.VMEM((rows, width), BF16)]


def first_call(rows, width, layout):
    full = 2 * width
    count = full // CHUNK
    half_shape = jax.ShapeDtypeStruct((rows, width), BF16)

    def kernel(*refs):
        first_kernel(layout, *refs)

    return pl.pallas_call(
        kernel,
        out_shape=(
            half_shape,
            half_shape,
            jax.ShapeDtypeStruct((full, width), BF16),
            jax.ShapeDtypeStruct((count, width, CHUNK), BF16),
        ),
        in_specs=[SMEM] + [VMEM] * 7 + [ANY] * len(layout),
        out_specs=(VMEM, VMEM, ANY, ANY),
        scratch_shapes=[pltpu.VMEM((rows, width), BF16)]
        + attention_scratch(rows, width)
        + [
            pltpu.VMEM((full, width), BF16),
            pltpu.VMEM((count, width, CHUNK), BF16),
            pltpu.SemaphoreType.DMA((len(layout) * SIDE,)),
            pltpu.SemaphoreType.DMA((1 + count,)),
        ],
        compiler_params=PARAMS,
        name="first_forward",
    )


def forward_call(rows, width):
    count = 2 * width // CHUNK
    half_shape = jax.ShapeDtypeStruct((rows, width), BF16)
    return pl.pallas_call(
        forward_kernel,
        out_shape=(half_shape, half_shape, half_shape),
        in_specs=[VMEM] * 7 + [ANY],
        out_specs=(VMEM, VMEM, VMEM),
        scratch_shapes=attention_scratch(rows, width)
        + [pltpu.VMEM((count, width, CHUNK), BF16), pltpu.SemaphoreType.DMA((count,))],
        compiler_params=PARAMS,
        name="layer_forward",
    )


def backward_call(rows, width):
    full = 2 * width
    heads = width // HEAD_DIM
    return pl.pallas_call(
        backward_kernel,
        out_shape=(
            jax.ShapeDtypeStruct((rows, width), F32),
            jax.ShapeDtypeStruct((rows, 1), F32),
        ),
        in_specs=[VMEM] * 7 + [ANY] + [VMEM] * 2,
        out_specs=(VMEM, VMEM),
        scratch_shapes=[
            pltpu.VMEM((full, width), BF16),
            pltpu.VMEM((heads, rows, rows), F32),
            pltpu.VMEM((heads, rows, rows), BF16),
            pltpu.VMEM((rows, width), BF16),
            pltpu.VMEM((rows, width), BF16),
            pltpu.VMEM((rows, width), BF16),
            pltpu.VMEM((rows, width), F32),
            pltpu.SemaphoreType.DMA((full // CHUNK,)),
        ],
        compiler_params=PARAMS,
        name="layer_backward",
    )


def weight_call(count, shard_pair, rows, width):
    shard = shard_pair // LAYERS_DEEP
    return pl.pallas_call(
        weight_kernel,
        out_shape=(
            jax.ShapeDtypeStruct((shard, width), F32),
            jax.ShapeDtypeStruct((shard, width), BF16),
        ),
        in_specs=[SMEM, VMEM, ANY],
        out_specs=(VMEM, VMEM),
        scratch_shapes=[
            pltpu.VMEM((count * rows, width), BF16),
            pltpu.VMEM((shard_pair, width), F32),
            pltpu.SemaphoreType.DMA((count,)),
        ],
        compiler_params=PARAMS,
        name="weight_gradient",
    )


def local(tokens_in, query_gain, key_gain, value_gain, out_weight, doc_lengths, grad_out):
    rows, width = tokens_in.shape
    full = 2 * width
    sections = lax.axis_size("section")
    section = lax.axis_index("section")
    half = lax.axis_index("tensor")
    index = lax.axis_index("dp")
    plane = index % LAYERS_DEEP
    x_at = index // LAYERS_DEEP % SIDE
    y_at = index // (LAYERS_DEEP * SIDE)
    place = jnp.stack([y_at, x_at, plane, half]).astype(jnp.int32)

    ends = jnp.cumsum(doc_lengths[0])
    ident = jnp.sum(
        (jnp.arange(rows, dtype=jnp.int32)[:, None] >= ends[None, :]).astype(jnp.int32), axis=1
    )
    fixed = (query_gain, key_gain, value_gain, ident[:, None], ident[None, :])

    def row_squares(block):
        wide = block.astype(F32)
        own = jnp.sum(wide * wide, axis=1, keepdims=True)
        return own + swap(own)

    first_squares = row_squares(tokens_in)
    pieces = gather_weight(out_weight[0].T)
    layout = tuple(piece[:3] for piece in pieces)

    x, squares = tokens_in, first_squares
    for turn in range(sections):
        if turn == 0:
            own, other, weight_rows, weight_cols = first_call(rows, width, layout)(
                place, x, squares, *fixed, *[piece[3] for piece in pieces]
            )
        else:
            own, other, mixed = forward_call(rows, width)(x, squares, *fixed, weight_cols)
        total = own.astype(F32) + swap(other).astype(F32)
        output = (x.astype(F32) + total).astype(BF16)
        if turn < sections - 1:
            arrived = relay(output, 1)
            arrived_squares = relay(row_squares(output), 1)
            x = jnp.where(section == 0, tokens_in, arrived)
            squares = jnp.where(section == 0, first_squares, arrived_squares)

    planes = [
        [grid_index(y, x, p) for y in range(SIDE) for x in range(SIDE)]
        for p in range(LAYERS_DEEP)
    ]
    mixed_all = lax.all_gather(mixed, "dp", axis_index_groups=planes, axis=0, tiled=True)

    backward = backward_call(rows, width)
    inverse = lax.rsqrt(squares / full + EPS)
    x_wide = x.astype(F32)
    grad = grad_out
    for turn in range(sections):
        pulled, inner = backward(x, squares, *fixed, weight_rows, grad, swap(grad))
        inner = inner + swap(inner)
        grad_in = (pulled - x_wide * (inner * inverse * inverse * inverse / full)).astype(BF16)
        if turn < sections - 1:
            arrived = relay(grad_in, -1)
            grad = jnp.where(section == sections - 1, grad_out, arrived)

    columns = exchange_columns(grad.T, y_at, x_at, half)
    columns = columns.reshape(SIDE * SIDE, -1, rows)
    near, far = weight_call(SIDE * SIDE, columns.shape[1], rows, width)(place, columns, mixed_all)
    weight_grads = (near + shift(far, "plane", 1).astype(F32)).T
    return output[None], grad_in[None], weight_grads[None]


def solution(mesh):
    return jax.shard_map(
        local,
        mesh=mesh,
        in_specs=(
            P("dp", "tensor"),
            P("section", "tensor"),
            P("section", "tensor"),
            P("section", "tensor"),
            P("section", "tensor", "dp"),
            P("dp", None),
            P("dp", "tensor"),
        ),
        out_specs=(
            P("section", "dp", "tensor"),
            P("section", "dp", "tensor"),
            P("section", "tensor", "dp"),
        ),
        check_vma=False,
    )
```

```python
import jax
import jax.numpy as jnp
from jax import lax
from jax.experimental import pallas as pl
from jax.experimental.pallas import tpu as pltpu
from jax.sharding import PartitionSpec as P

HEAD_DIM = 128
EPS = 1e-05
CHUNK = 256
SIDE = 4
PLANES = 2
F32 = jnp.float32
BF16 = jnp.bfloat16
NN = (((1,), (0,)), ((), ()))
NT = (((1,), (1,)), ((), ()))
TN = (((0,), (0,)), ((), ()))
MIB = 1024 * 1024
FIRST_OFFSETS = (0, -1, -2, 1)


def dot(a, b, dims):
    return lax.dot_general(a, b, dims, preferred_element_type=F32)


def split(a):
    high = a.astype(BF16)
    return high, (a - high.astype(F32)).astype(BF16)


def grid_index(y, x, plane):
    return ((y % SIDE) * SIDE + x % SIDE) * PLANES + plane % PLANES


def shift(block, axis, step):
    move = {"y": (step, 0, 0), "x": (0, step, 0), "plane": (0, 0, step)}[axis]
    route = [
        (grid_index(y, x, p), grid_index(y + move[0], x + move[1], p + move[2]))
        for y in range(SIDE)
        for x in range(SIDE)
        for p in range(PLANES)
    ]
    return lax.ppermute(block, "dp", route)


def tied(blocks, *others):
    return list(lax.optimization_barrier(tuple(blocks) + tuple(others))[: len(blocks)])


def gather_weight(shard):
    width = shard.shape[1] // 2
    sides = ((slice(0, width), "x", "y"), (slice(width, 2 * width), "y", "x"))
    seconds = [side[2] for side in sides]

    def first_ring(block):
        own = [block[:, side[0]] for side in sides]
        backs = [shift(part, side[1], 1) for part, side in zip(own, sides)]
        aheads = [shift(part, side[1], -1) for part, side in zip(own, sides)]
        across = [shift(part, side[1], 1) for part, side in zip(backs, sides)]
        joined = [jnp.concatenate(parts, axis=0) for parts in zip(own, backs, across, aheads)]
        return joined, backs + aheads

    def both(blocks, step):
        return [shift(block, axis, step) for block, axis in zip(blocks, seconds)]

    near, firsts = first_ring(shard)
    sent, *firsts = lax.optimization_barrier((shard, *firsts))
    far_shard = shift(sent, "plane", 1)
    near = tied(near)
    near_back, near_ahead = both(near, 1), both(near, -1)
    far, _ = first_ring(far_shard)
    near_back = tied(near_back)
    near_across = both(near_back, 1)
    far = tied(far, *near_back, *near_ahead)
    far_ahead = both(far, -1)
    late = tied(far, *near_across)
    far_back = both(late, 1)
    far_across = both(far_ahead, -1)
    pieces = []
    for side in range(2):
        for plane, group in enumerate(
            ((near, near_back, near_ahead, near_across), (far, far_back, far_ahead, far_across))
        ):
            for offset, blocks in zip((0, -1, 1, -2), group):
                pieces.append((side, plane, offset, blocks[side]))
    return pieces


def exchange_columns(place, is_last, given, arrived, mixed_all):
    rows, width = given.shape
    size = width // (2 * SIDE)
    chunks = call(
        columns_kernel,
        [((2, size, rows), BF16)] * SIDE,
        [SMEM, SMEM, VMEM, VMEM],
        [pltpu.VMEM((width, rows), BF16)],
        "cut_columns",
        12,
    )(place, is_last, given, arrived)
    parts = [shift(chunk, "x", step) if step else chunk for step, chunk in enumerate(chunks)]
    parts = call(
        pick_kernel,
        [((SIDE, size, rows), BF16)] * SIDE,
        [SMEM] + [VMEM] * SIDE,
        [],
        "pick_columns",
        12,
    )(place, *parts)
    ordered, token = call(
        order_kernel,
        [(mixed_all.shape, BF16), ((8, HEAD_DIM), F32)],
        [SMEM, ANY],
        [pltpu.SemaphoreType.DMA((SIDE * SIDE,))],
        "order_mixed",
        40,
    )(place, tied([mixed_all], *parts)[0])
    result = []
    for step, part in enumerate(parts):
        if step:
            route = []
            for row in range(SIDE):
                target = (row + step) % SIDE
                for col in range(SIDE):
                    for p in range(PLANES):
                        source, sink = grid_index(row, col, p), grid_index(target, col, p)
                        route.append((source * 2 + target // 2, sink * 2 + target // 2))
            part = lax.ppermute(part, ("dp", "tensor"), route)
        result.append(part)
    *result, token = lax.optimization_barrier((*result, token))
    return result + [swap(part) for part in result] + [token], ordered


def swap(block):
    return lax.ppermute(block, "tensor", [(0, 1), (1, 0)])


def relay(block, step):
    sections = lax.axis_size("section")
    route = [(i, i + step) for i in range(sections) if 0 <= i + step < sections]
    return lax.ppermute(block, "section", route)


def allowed_mask(id_col, id_row):
    shape = (id_col.shape[0], id_row.shape[1])
    rows = lax.broadcasted_iota(jnp.int32, shape, 0)
    cols = lax.broadcasted_iota(jnp.int32, shape, 1)
    return (rows >= cols) & (id_col[...] == id_row[...])


def softmax(scores, allowed):
    scores = jnp.where(allowed, scores * HEAD_DIM**-0.5, -1e30)
    expo = jnp.exp(scores - jnp.max(scores, axis=1, keepdims=True))
    return expo / jnp.sum(expo, axis=1, keepdims=True)


def head_slices(width):
    return [slice(i, i + HEAD_DIM) for i in range(0, width, HEAD_DIM)]


def attend(x_ref, inverse, gq_ref, gk_ref, gv_ref, id_col, id_row, probs_buf, values_buf, mixed_ref):
    allowed = allowed_mask(id_col, id_row)
    heads = head_slices(x_ref.shape[1])
    for head, cols in enumerate(heads):
        normed = x_ref[:, cols].astype(F32) * inverse
        queries = (normed * gq_ref[:, cols]).astype(BF16)
        keys = (normed * gk_ref[:, cols]).astype(BF16)
        values_buf[:, cols] = (normed * gv_ref[:, cols]).astype(BF16)
        probs_buf[head] = softmax(dot(queries, keys, NT), allowed).astype(BF16)
    for head, cols in enumerate(heads):
        mixed_ref[:, cols] = dot(probs_buf[head], values_buf[:, cols], NN).astype(BF16)


def inverse_norm(squares_ref, squares_other_ref, full):
    return lax.rsqrt((squares_ref[...] + squares_other_ref[...]) / full + EPS)


def start_all(copies):
    for copy in copies:
        copy.start()


def attention_kernel(x_ref, squares_ref, squares_other_ref, *refs):
    inverse = inverse_norm(squares_ref, squares_other_ref, 2 * x_ref.shape[1])
    fixed, (mixed_ref, probs_buf, values_buf) = refs[:5], refs[5:]
    attend(x_ref, inverse, *fixed, probs_buf, values_buf, mixed_ref)


def first_kernel(layout, place_ref, x_ref, mixed_ref, *refs):
    pieces, refs = refs[: len(layout)], refs[len(layout) :]
    base_ref, other_ref, rows_out, held, product, sems, out_sems = refs
    y, x, plane, half = [place_ref[i] for i in range(4)]
    full, width = held.shape
    shard = pieces[0].shape[0] // SIDE
    groups = [[] for _ in range(SIDE)]
    for (side, far, offset), piece in zip(layout, pieces):
        for part, first in enumerate(FIRST_OFFSETS):
            at_y, at_x = (offset, first) if side == 0 else (first, offset)
            row = lax.rem(y + at_y + SIDE, SIDE)
            col = lax.rem(x + at_x + SIDE, SIDE)
            depth = 1 - plane if far else plane
            start = lax.rem(((row * SIDE + col) * PLANES + depth) * shard + half * width, full)
            start = pl.multiple_of(start, 16)
            group = groups[-at_y % SIDE]
            group.append(
                pltpu.make_async_copy(
                    piece.at[pl.ds(part * shard, shard)],
                    held.at[pl.ds(start, shard), pl.ds(side * (width // 2), width // 2)],
                    sems.at[-at_y % SIDE, len(group)],
                )
            )
    for group in groups:
        start_all(group)
    mixed = mixed_ref[...]
    block = full // SIDE
    outs = []
    for step, group in enumerate(groups):
        for copy in group:
            copy.wait()
        start = lax.rem(lax.rem(y - step + SIDE, SIDE) * block + half * width, full)
        start = pl.multiple_of(start, HEAD_DIM)
        rows = pl.ds(start, block)
        outs.append(pltpu.make_async_copy(held.at[rows], rows_out.at[rows], out_sems.at[step]))
        outs[-1].start()
        for i in range(0, block, CHUNK):
            at = pl.multiple_of(start + i, HEAD_DIM)
            size = min(CHUNK, block - i)
            part = dot(mixed, held[pl.ds(at, size), :], NT)
            product[:, pl.ds(at, size)] = part.astype(BF16)
    base_ref[...] = x_ref[...].astype(F32) + product[:, :width].astype(F32)
    other_ref[...] = product[:, width:]
    for out in outs:
        out.wait()


def turn_kernel(rows_ref, cols_ref, token_ref):
    token_ref[...] = jnp.zeros_like(token_ref)
    for i in range(0, rows_ref.shape[0], CHUNK):
        cols_ref[:, i : i + CHUNK] = rows_ref[i : i + CHUNK, :].T


def output_kernel(base_ref, other_ref, out_ref):
    out_ref[...] = (base_ref[...] + other_ref[...].astype(F32)).astype(BF16)


def squares_kernel(x_ref, out_ref):
    total = jnp.zeros((x_ref.shape[0], HEAD_DIM), F32)
    for cols in head_slices(x_ref.shape[1]):
        part = x_ref[:, cols].astype(F32)
        total = total + part * part
    out_ref[...] = jnp.sum(total, axis=1, keepdims=True)


def columns_kernel(place_ref, is_last, given_ref, arrived_ref, *refs):
    outs, turned = refs[:-1], refs[-1]

    @pl.when(is_last[0] == 1)
    def _():
        turned[...] = given_ref[...].T

    @pl.when(is_last[0] == 0)
    def _():
        turned[...] = arrived_ref[...].T

    size = outs[0].shape[1]
    for step, out in enumerate(outs):
        col = lax.rem(place_ref[1] + step, SIDE)
        for i in range(2):
            start = pl.multiple_of((i * SIDE + col) * size, 16)
            out[i] = turned[pl.ds(start, size), :]


def pick_kernel(place_ref, *refs):
    parts, outs = refs[:SIDE], refs[SIDE:]
    for step, out in enumerate(outs):
        which = lax.rem(place_ref[0] + step, 2)
        for i, part in enumerate(parts):
            out[i] = part[which]


def forward_kernel(
    is_first, tokens_ref, tokens_squares, tokens_squares_other, arrived_ref, squares_ref,
    squares_other_ref, *refs,
):
    fixed, refs = refs[:5], refs[6:]
    cols_ref, base_ref, other_ref, mixed_ref, x_ref, total_ref, probs_buf, values_buf = refs

    @pl.when(is_first[0] == 1)
    def _():
        x_ref[...] = tokens_ref[...]
        total_ref[...] = tokens_squares[...] + tokens_squares_other[...]

    @pl.when(is_first[0] == 0)
    def _():
        x_ref[...] = arrived_ref[...]
        total_ref[...] = squares_ref[...] + squares_other_ref[...]

    width = x_ref.shape[1]
    inverse = lax.rsqrt(total_ref[...] / (2 * width) + EPS)
    attend(x_ref, inverse, *fixed, probs_buf, values_buf, mixed_ref)
    mixed = mixed_ref[...]
    for i in range(0, width, CHUNK):
        cols = slice(i, i + CHUNK)
        own = dot(mixed, cols_ref[:, cols], NN).astype(BF16)
        base_ref[:, cols] = x_ref[:, cols].astype(F32) + own.astype(F32)
        other_ref[:, cols] = dot(mixed, cols_ref[:, width + i : width + i + CHUNK], NN).astype(BF16)


def prepare_kernel(
    x_ref, total_ref, gq_ref, gk_ref, gv_ref, id_col, id_row, probs_ref, q_ref, k_ref, v_ref
):
    width = x_ref.shape[1]
    inverse = lax.rsqrt(total_ref[...] / (2 * width) + EPS)
    allowed = allowed_mask(id_col, id_row)
    for head, cols in enumerate(head_slices(width)):
        normed = x_ref[:, cols].astype(F32) * inverse
        q_high, q_low = split(normed * gq_ref[:, cols])
        k_high, k_low = split(normed * gk_ref[:, cols])
        q_ref[:, cols] = q_high
        k_ref[:, cols] = k_high
        v_ref[:, cols] = (normed * gv_ref[:, cols]).astype(BF16)
        scores = dot(
            jnp.concatenate([q_high, q_high, q_low], axis=1),
            jnp.concatenate([k_high, k_low, k_high], axis=1),
            NT,
        )
        probs_ref[head] = softmax(scores, allowed)


def backward_kernel(
    is_last, given_ref, given_other_ref, arrived_ref, arrived_other_ref, x_ref, total_ref, gq_ref,
    gk_ref, gv_ref, probs_ref, q_ref, k_ref, v_ref, rows_ref, sum_ref, inner_ref, grad_buf,
    mixed_buf, scores_buf,
):
    full, width = rows_ref.shape

    @pl.when(is_last[0] == 1)
    def _():
        grad_buf[:, :width] = given_ref[...]
        grad_buf[:, width:] = given_other_ref[...]

    @pl.when(is_last[0] == 0)
    def _():
        grad_buf[:, :width] = arrived_ref[...]
        grad_buf[:, width:] = arrived_other_ref[...]

    inverse = lax.rsqrt(total_ref[...] / full + EPS)
    heads = head_slices(width)
    for i in range(0, width, CHUNK):
        cols = slice(i, i + CHUNK)
        mixed_buf[:, cols] = dot(grad_buf[...], rows_ref[:, cols], NN).astype(BF16)
    for head, cols in enumerate(heads):
        probs = probs_ref[head]
        weighted = probs * dot(mixed_buf[:, cols], v_ref[:, cols], NT)
        inner = jnp.sum(weighted, axis=1, keepdims=True)
        scores_buf[head] = ((weighted - probs * inner) * HEAD_DIM**-0.5).astype(BF16)
    inner = jnp.zeros((x_ref.shape[0], HEAD_DIM), F32)
    for head, cols in enumerate(heads):
        grad_scores = scores_buf[head]
        grad_values = dot(probs_ref[head].astype(BF16), mixed_buf[:, cols], TN)
        grad_normed = (
            dot(grad_scores, k_ref[:, cols], NN) * gq_ref[:, cols]
            + dot(grad_scores, q_ref[:, cols], TN) * gk_ref[:, cols]
            + grad_values * gv_ref[:, cols]
        )
        inner = inner + grad_normed * x_ref[:, cols].astype(F32)
        sum_ref[:, cols] = grad_buf[:, cols].astype(F32) + grad_normed * inverse
    inner_ref[...] = jnp.sum(inner, axis=1, keepdims=True)


def finish_kernel(sum_ref, inner_ref, inner_other_ref, x_ref, total_ref, out_ref):
    full = 2 * x_ref.shape[1]
    inverse = lax.rsqrt(total_ref[...] / full + EPS)
    inner = inner_ref[...] + inner_other_ref[...]
    factor = inner * inverse * inverse * inverse / full
    out_ref[...] = (sum_ref[...] - x_ref[...].astype(F32) * factor).astype(BF16)


def order_kernel(place_ref, mixed_ref, held_ref, token_ref, sems):
    token_ref[...] = jnp.zeros_like(token_ref)
    count = sems.shape[0]
    rows = mixed_ref.shape[0] // count
    copies = []
    for i in range(count):
        row = lax.rem(place_ref[0] - i // SIDE + SIDE, SIDE)
        col = lax.rem(place_ref[1] - i % SIDE + SIDE, SIDE)
        source = pl.multiple_of((row * SIDE + col) * rows, rows)
        target = held_ref.at[pl.ds(i * rows, rows)]
        copies.append(
            pltpu.make_async_copy(mixed_ref.at[pl.ds(source, rows)], target, sems.at[i])
        )
    start_all(copies)
    for copy in copies:
        copy.wait()


def weight_kernel(place_ref, *refs):
    columns, (mixed_ref, own_ref, far_ref, total) = refs[: 2 * SIDE], refs[2 * SIDE + 1 :]
    plane = place_ref[2]
    shard = own_ref.shape[0]
    size = mixed_ref.shape[0] // SIDE
    here = jnp.full(columns[0].shape[1:], place_ref[0] // 2 == place_ref[3])
    for i in range(SIDE):
        blocks = [jnp.where(here, columns[i][j], columns[SIDE + i][j]) for j in range(SIDE)]
        part = dot(jnp.concatenate(blocks, axis=1), mixed_ref[i * size : (i + 1) * size], NN)
        total[...] = part if i == 0 else total[...] + part
    own_ref[...] = total[pl.ds(pl.multiple_of(plane * shard, 16), shard)]
    far_ref[...] = total[pl.ds(pl.multiple_of((1 - plane) * shard, 16), shard)].astype(BF16)


VMEM = pl.BlockSpec(memory_space=pltpu.VMEM)
SMEM = pl.BlockSpec(memory_space=pltpu.SMEM)
ANY = pl.BlockSpec(memory_space=pl.ANY)


def call(kernel, outs, in_specs, scratch, name, limit, out_specs=None):
    return pl.pallas_call(
        kernel,
        out_shape=tuple(jax.ShapeDtypeStruct(shape, kind) for shape, kind in outs),
        in_specs=in_specs,
        out_specs=out_specs or (VMEM,) * len(outs),
        scratch_shapes=scratch,
        compiler_params=pltpu.CompilerParams(vmem_limit_bytes=limit * MIB),
        name=name,
    )


def local(tokens_in, query_gain, key_gain, value_gain, out_weight, doc_lengths, grad_out):
    rows, width = tokens_in.shape
    full = 2 * width
    heads = width // HEAD_DIM
    shard = out_weight.shape[2]
    sections = lax.axis_size("section")
    section = lax.axis_index("section")
    half = lax.axis_index("tensor")
    index = lax.axis_index("dp")
    plane = index % PLANES
    x_at = index // PLANES % SIDE
    y_at = index // (PLANES * SIDE)
    place = jnp.stack([y_at, x_at, plane, half]).astype(jnp.int32)
    is_first = (section == 0).astype(jnp.int32).reshape(1)
    is_last = (section == sections - 1).astype(jnp.int32).reshape(1)

    ends = jnp.cumsum(doc_lengths[0])
    ident = jnp.sum(
        (jnp.arange(rows, dtype=jnp.int32)[:, None] >= ends[None, :]).astype(jnp.int32), axis=1
    )
    gains = (query_gain, key_gain, value_gain)
    fixed = gains + (ident[:, None], ident[None, :])
    block, column = (rows, width), (rows, 1)
    buffers = [pltpu.VMEM((heads, rows, rows), BF16), pltpu.VMEM(block, BF16)]

    def row_squares(part):
        own = call(squares_kernel, [(column, F32)], [VMEM], [], "row_squares", 8)(part)[0]
        return own, swap(own)

    def summed(base, other):
        shape = [(block, BF16)]
        return call(output_kernel, shape, [VMEM] * 2, [], "layer_output", 8)(base, swap(other))[0]

    first_squares = row_squares(tokens_in)
    (mixed,) = call(
        attention_kernel, [(block, BF16)], [VMEM] * 8, buffers, "first_attention", 12
    )(tokens_in, *first_squares, *fixed)
    pieces = gather_weight(out_weight[0].T)
    layout = tuple(piece[:3] for piece in pieces)
    base, other, weight_rows = call(
        lambda *refs: first_kernel(layout, *refs),
        [(block, F32), (block, BF16), ((full, width), BF16)],
        [SMEM, VMEM, VMEM] + [ANY] * len(layout),
        [
            pltpu.VMEM((full, width), BF16),
            pltpu.VMEM((rows, full), BF16),
            pltpu.SemaphoreType.DMA((SIDE, len(layout))),
            pltpu.SemaphoreType.DMA((SIDE,)),
        ],
        "first_forward",
        58,
        (VMEM, VMEM, ANY),
    )(place, tokens_in, mixed, *[piece[3] for piece in pieces])
    output = summed(base, other)
    (weight_rows,) = tied([weight_rows], output)
    token = ((8, HEAD_DIM), F32)
    weight_cols, turned = call(
        turn_kernel, [((width, full), BF16), token], [VMEM], [], "turn_weight", 28
    )(weight_rows)

    forward = call(
        forward_kernel,
        [(block, F32), (block, BF16), (block, BF16), (block, BF16), (column, F32)],
        [SMEM] + [VMEM] * 13,
        buffers,
        "layer_forward",
        20,
    )
    for turn in range(1, sections):
        arrived = relay(output, 1)
        if turn == 1:
            arrived, ready = lax.optimization_barrier((arrived, turned))
        base, other, mixed, x, squares = forward(
            is_first, tokens_in, *first_squares, arrived, *row_squares(arrived), *fixed, ready, weight_cols
        )
        output = summed(base, other)

    planes = [
        [grid_index(y, x, p) for y in range(SIDE) for x in range(SIDE)] for p in range(PLANES)
    ]
    mixed_all = lax.all_gather(mixed, "dp", axis_index_groups=planes, axis=0, tiled=True)
    probs, queries, keys, values = call(
        prepare_kernel,
        [((heads, rows, rows), F32), (block, BF16), (block, BF16), (block, BF16)],
        [VMEM] * 7,
        [],
        "backward_probs",
        12,
    )(x, squares, *fixed)
    backward = call(
        backward_kernel,
        [(block, F32), (column, F32)],
        [SMEM] + [VMEM] * 14,
        [
            pltpu.VMEM((rows, full), BF16),
            pltpu.VMEM(block, BF16),
            pltpu.VMEM((heads, rows, rows), BF16),
        ],
        "layer_backward",
        22,
    )
    finish = call(finish_kernel, [(block, BF16)], [VMEM] * 5, [], "input_gradient", 8)
    given = (grad_out, swap(grad_out))

    def input_gradient(arrived, held):
        pulled, inner = backward(
            is_last, *given, *arrived, x, squares, *gains, probs, queries, keys, values, held
        )
        return finish(pulled, inner, swap(inner), x, squares)[0]

    def passed(grad_in):
        grad = relay(grad_in, -1)
        return grad, swap(grad)

    grad_in = input_gradient(given, weight_rows)
    for turn in range(1, sections - 1):
        grad_in = input_gradient(passed(grad_in), weight_rows)
    arrived = passed(grad_in)

    columns, ordered = exchange_columns(place, is_last, grad_out, arrived[0], mixed_all)
    near, far = call(
        weight_kernel,
        [((shard, width), F32), ((shard, width), BF16)],
        [SMEM] + [VMEM] * (2 * SIDE + 2),
        [pltpu.VMEM((PLANES * shard, width), F32)],
        "weight_gradient",
        24,
    )(place, *columns, ordered)
    far_sum = shift(far, "plane", 1)
    grad_in = input_gradient(tied(arrived, far), weight_rows)
    weight_grads = (near + far_sum.astype(F32)).T
    return output[None], grad_in[None], weight_grads[None]


def solution(mesh):
    return jax.shard_map(
        local,
        mesh=mesh,
        in_specs=(
            P("dp", "tensor"),
            P("section", "tensor"),
            P("section", "tensor"),
            P("section", "tensor"),
            P("section", "tensor", "dp"),
            P("dp", None),
            P("dp", "tensor"),
        ),
        out_specs=(
            P("section", "dp", "tensor"),
            P("section", "dp", "tensor"),
            P("section", "tensor", "dp"),
        ),
        check_vma=False,
    )
```

```python
import jax
import jax.numpy as jnp
from jax import lax
from jax.experimental import pallas as pl
from jax.experimental.pallas import tpu as pltpu
from jax.sharding import PartitionSpec as P

HEAD_DIM = 128
EPS = 1e-05
CHUNK = 256
SIDE = 4
PLANES = 2
F32 = jnp.float32
BF16 = jnp.bfloat16
NN = (((1,), (0,)), ((), ()))
NT = (((1,), (1,)), ((), ()))
TN = (((0,), (0,)), ((), ()))
MIB = 1024 * 1024
FIRST_OFFSETS = (0, -1, -2, 1)


def dot(a, b, dims):
    return lax.dot_general(a, b, dims, preferred_element_type=F32)


def split(a):
    high = a.astype(BF16)
    return high, (a - high.astype(F32)).astype(BF16)


def grid_index(y, x, plane):
    return ((y % SIDE) * SIDE + x % SIDE) * PLANES + plane % PLANES


def shift(block, axis, step):
    move = {"y": (step, 0, 0), "x": (0, step, 0), "plane": (0, 0, step)}[axis]
    route = [
        (grid_index(y, x, p), grid_index(y + move[0], x + move[1], p + move[2]))
        for y in range(SIDE)
        for x in range(SIDE)
        for p in range(PLANES)
    ]
    return lax.ppermute(block, "dp", route)


def tied(blocks, *others):
    return list(lax.optimization_barrier(tuple(blocks) + tuple(others))[: len(blocks)])


def gather_weight(shard):
    width = shard.shape[1] // 2
    sides = ((slice(0, width), "x", "y"), (slice(width, 2 * width), "y", "x"))
    seconds = [side[2] for side in sides]

    def first_ring(block):
        joined = []
        for cols, axis, _ in sides:
            own = block[:, cols]
            back, ahead = shift(own, axis, 1), shift(own, axis, -1)
            joined.append(jnp.concatenate([own, back, shift(back, axis, 1), ahead], axis=0))
        return joined

    def both(blocks, step):
        return [shift(block, axis, step) for block, axis in zip(blocks, seconds)]

    far_shard = shift(shard, "plane", 1)
    near = tied(first_ring(shard))
    near_back, near_ahead = both(near, 1), both(near, -1)
    far_shard, *moved = lax.optimization_barrier((far_shard, *near_back, *near_ahead))
    near_back, near_ahead = moved[:2], moved[2:]
    near_across = both(near_back, 1)
    far = tied(first_ring(far_shard))
    far_ahead = both(far, -1)
    late = tied(far, *near_across)
    far_back = both(late, 1)
    far_across = both(far_ahead, -1)
    pieces = []
    for side in range(2):
        for plane, group in enumerate(
            ((near, near_back, near_ahead, near_across), (far, far_back, far_ahead, far_across))
        ):
            for offset, blocks in zip((0, -1, 1, -2), group):
                pieces.append((side, plane, offset, blocks[side]))
    return pieces


def exchange_columns(place, is_last, given, arrived, mixed_all):
    rows, width = given.shape
    size = width // (2 * SIDE)
    chunks = call(
        columns_kernel,
        [((2, size, rows), BF16)] * SIDE,
        [SMEM, SMEM, VMEM, VMEM],
        [pltpu.VMEM((width, rows), BF16)],
        "cut_columns",
        12,
    )(place, is_last, given, arrived)
    ordered, token = call(
        order_kernel,
        [(mixed_all.shape, BF16), ((8, HEAD_DIM), F32)],
        [SMEM, ANY],
        [pltpu.SemaphoreType.DMA((SIDE * SIDE,))],
        "order_mixed",
        40,
    )(place, tied([mixed_all], *chunks)[0])
    parts = [shift(chunk, "x", step) if step else chunk for step, chunk in enumerate(chunks)]
    *parts, token = lax.optimization_barrier((*parts, token))
    parts = call(
        pick_kernel,
        [((SIDE, size, rows), BF16)] * SIDE,
        [SMEM] + [VMEM] * (SIDE + 1),
        [],
        "pick_columns",
        12,
    )(place, token, *parts)
    result = []
    for step, part in enumerate(parts):
        if step:
            route = []
            for row in range(SIDE):
                target = (row + step) % SIDE
                for col in range(SIDE):
                    for p in range(PLANES):
                        source, sink = grid_index(row, col, p), grid_index(target, col, p)
                        route.append((source * 2 + target // 2, sink * 2 + target // 2))
            part = lax.ppermute(part, ("dp", "tensor"), route)
        result.append(part)
    return result + [swap(part) for part in result], ordered


def swap(block):
    return lax.ppermute(block, "tensor", [(0, 1), (1, 0)])


def relay(block, step):
    sections = lax.axis_size("section")
    route = [(i, i + step) for i in range(sections) if 0 <= i + step < sections]
    return lax.ppermute(block, "section", route)


def allowed_mask(id_col, id_row):
    shape = (id_col.shape[0], id_row.shape[1])
    rows = lax.broadcasted_iota(jnp.int32, shape, 0)
    cols = lax.broadcasted_iota(jnp.int32, shape, 1)
    return (rows >= cols) & (id_col[...] == id_row[...])


def softmax(scores, allowed):
    scores = jnp.where(allowed, scores * HEAD_DIM**-0.5, -1e30)
    expo = jnp.exp(scores - jnp.max(scores, axis=1, keepdims=True))
    return expo / jnp.sum(expo, axis=1, keepdims=True)


def head_slices(width):
    return [slice(i, i + HEAD_DIM) for i in range(0, width, HEAD_DIM)]


def attend(x_ref, inverse, gq_ref, gk_ref, gv_ref, id_col, id_row, probs_buf, values_buf, mixed_ref):
    allowed = allowed_mask(id_col, id_row)
    heads = head_slices(x_ref.shape[1])
    for head, cols in enumerate(heads):
        normed = x_ref[:, cols].astype(F32) * inverse
        queries = (normed * gq_ref[:, cols]).astype(BF16)
        keys = (normed * gk_ref[:, cols]).astype(BF16)
        values_buf[:, cols] = (normed * gv_ref[:, cols]).astype(BF16)
        probs_buf[head] = softmax(dot(queries, keys, NT), allowed).astype(BF16)
    for head, cols in enumerate(heads):
        mixed_ref[:, cols] = dot(probs_buf[head], values_buf[:, cols], NN).astype(BF16)


def inverse_norm(squares_ref, squares_other_ref, full):
    return lax.rsqrt((squares_ref[...] + squares_other_ref[...]) / full + EPS)


def start_all(copies):
    for copy in copies:
        copy.start()


def attention_kernel(x_ref, squares_ref, squares_other_ref, *refs):
    inverse = inverse_norm(squares_ref, squares_other_ref, 2 * x_ref.shape[1])
    fixed, (mixed_ref, probs_buf, values_buf) = refs[:5], refs[5:]
    attend(x_ref, inverse, *fixed, probs_buf, values_buf, mixed_ref)


def first_kernel(layout, place_ref, x_ref, mixed_ref, *refs):
    pieces, refs = refs[: len(layout)], refs[len(layout) :]
    base_ref, other_ref, rows_out, held, product, sems, out_sems = refs
    y, x, plane, half = [place_ref[i] for i in range(4)]
    full, width = held.shape
    shard = pieces[0].shape[0] // SIDE
    groups = [[] for _ in range(SIDE)]
    for (side, far, offset), piece in zip(layout, pieces):
        for part, first in enumerate(FIRST_OFFSETS):
            at_y, at_x = (offset, first) if side == 0 else (first, offset)
            row = lax.rem(y + at_y + SIDE, SIDE)
            col = lax.rem(x + at_x + SIDE, SIDE)
            depth = 1 - plane if far else plane
            start = lax.rem(((row * SIDE + col) * PLANES + depth) * shard + half * width, full)
            start = pl.multiple_of(start, 16)
            group = groups[-at_y % SIDE]
            group.append(
                pltpu.make_async_copy(
                    piece.at[pl.ds(part * shard, shard)],
                    held.at[pl.ds(start, shard), pl.ds(side * (width // 2), width // 2)],
                    sems.at[-at_y % SIDE, len(group)],
                )
            )
    for group in groups:
        start_all(group)
    mixed = mixed_ref[...]
    block = full // SIDE
    outs = []
    for step, group in enumerate(groups):
        for copy in group:
            copy.wait()
        start = lax.rem(lax.rem(y - step + SIDE, SIDE) * block + half * width, full)
        start = pl.multiple_of(start, HEAD_DIM)
        rows = pl.ds(start, block)
        outs.append(pltpu.make_async_copy(held.at[rows], rows_out.at[rows], out_sems.at[step]))
        outs[-1].start()
        for i in range(0, block, CHUNK):
            at = pl.multiple_of(start + i, HEAD_DIM)
            size = min(CHUNK, block - i)
            part = dot(mixed, held[pl.ds(at, size), :], NT)
            product[:, pl.ds(at, size)] = part.astype(BF16)
    base_ref[...] = x_ref[...].astype(F32) + product[:, :width].astype(F32)
    other_ref[...] = product[:, width:]
    for out in outs:
        out.wait()


def turn_kernel(rows_ref, cols_ref, token_ref):
    token_ref[...] = jnp.zeros_like(token_ref)
    for i in range(0, rows_ref.shape[0], CHUNK):
        cols_ref[:, i : i + CHUNK] = rows_ref[i : i + CHUNK, :].T


def output_kernel(base_ref, other_ref, out_ref):
    out_ref[...] = (base_ref[...] + other_ref[...].astype(F32)).astype(BF16)


def squares_kernel(x_ref, out_ref):
    total = jnp.zeros((x_ref.shape[0], HEAD_DIM), F32)
    for cols in head_slices(x_ref.shape[1]):
        part = x_ref[:, cols].astype(F32)
        total = total + part * part
    out_ref[...] = jnp.sum(total, axis=1, keepdims=True)


def columns_kernel(place_ref, is_last, given_ref, arrived_ref, *refs):
    outs, turned = refs[:-1], refs[-1]

    @pl.when(is_last[0] == 1)
    def _():
        turned[...] = given_ref[...].T

    @pl.when(is_last[0] == 0)
    def _():
        turned[...] = arrived_ref[...].T

    size = outs[0].shape[1]
    for step, out in enumerate(outs):
        col = lax.rem(place_ref[1] + step, SIDE)
        for i in range(2):
            start = pl.multiple_of((i * SIDE + col) * size, 16)
            out[i] = turned[pl.ds(start, size), :]


def pick_kernel(place_ref, token_ref, *refs):
    parts, outs = refs[:SIDE], refs[SIDE:]
    for step, out in enumerate(outs):
        which = lax.rem(place_ref[0] + step, 2)
        for i, part in enumerate(parts):
            out[i] = part[which]


def forward_kernel(
    is_first, tokens_ref, tokens_squares, tokens_squares_other, arrived_ref, squares_ref,
    squares_other_ref, *refs,
):
    fixed, refs = refs[:5], refs[6:]
    cols_ref, base_ref, other_ref, mixed_ref, x_ref, total_ref, probs_buf, values_buf = refs

    @pl.when(is_first[0] == 1)
    def _():
        x_ref[...] = tokens_ref[...]
        total_ref[...] = tokens_squares[...] + tokens_squares_other[...]

    @pl.when(is_first[0] == 0)
    def _():
        x_ref[...] = arrived_ref[...]
        total_ref[...] = squares_ref[...] + squares_other_ref[...]

    width = x_ref.shape[1]
    inverse = lax.rsqrt(total_ref[...] / (2 * width) + EPS)
    attend(x_ref, inverse, *fixed, probs_buf, values_buf, mixed_ref)
    mixed = mixed_ref[...]
    for i in range(0, width, CHUNK):
        cols = slice(i, i + CHUNK)
        own = dot(mixed, cols_ref[:, cols], NN).astype(BF16)
        base_ref[:, cols] = x_ref[:, cols].astype(F32) + own.astype(F32)
        other_ref[:, cols] = dot(mixed, cols_ref[:, width + i : width + i + CHUNK], NN).astype(BF16)


def prepare_kernel(
    x_ref, total_ref, gq_ref, gk_ref, gv_ref, id_col, id_row, probs_ref, q_ref, k_ref, v_ref
):
    width = x_ref.shape[1]
    inverse = lax.rsqrt(total_ref[...] / (2 * width) + EPS)
    allowed = allowed_mask(id_col, id_row)
    for head, cols in enumerate(head_slices(width)):
        normed = x_ref[:, cols].astype(F32) * inverse
        q_high, q_low = split(normed * gq_ref[:, cols])
        k_high, k_low = split(normed * gk_ref[:, cols])
        q_ref[:, cols] = q_high
        k_ref[:, cols] = k_high
        v_ref[:, cols] = (normed * gv_ref[:, cols]).astype(BF16)
        scores = dot(
            jnp.concatenate([q_high, q_high, q_low], axis=1),
            jnp.concatenate([k_high, k_low, k_high], axis=1),
            NT,
        )
        probs_ref[head] = softmax(scores, allowed)


def backward_kernel(
    is_last, given_ref, given_other_ref, arrived_ref, arrived_other_ref, x_ref, total_ref, gq_ref,
    gk_ref, gv_ref, probs_ref, q_ref, k_ref, v_ref, rows_ref, sum_ref, inner_ref, grad_buf,
    mixed_buf, scores_buf,
):
    full, width = rows_ref.shape

    @pl.when(is_last[0] == 1)
    def _():
        grad_buf[:, :width] = given_ref[...]
        grad_buf[:, width:] = given_other_ref[...]

    @pl.when(is_last[0] == 0)
    def _():
        grad_buf[:, :width] = arrived_ref[...]
        grad_buf[:, width:] = arrived_other_ref[...]

    inverse = lax.rsqrt(total_ref[...] / full + EPS)
    heads = head_slices(width)
    for i in range(0, width, CHUNK):
        cols = slice(i, i + CHUNK)
        mixed_buf[:, cols] = dot(grad_buf[...], rows_ref[:, cols], NN).astype(BF16)
    for head, cols in enumerate(heads):
        probs = probs_ref[head]
        weighted = probs * dot(mixed_buf[:, cols], v_ref[:, cols], NT)
        inner = jnp.sum(weighted, axis=1, keepdims=True)
        scores_buf[head] = ((weighted - probs * inner) * HEAD_DIM**-0.5).astype(BF16)
    inner = jnp.zeros((x_ref.shape[0], HEAD_DIM), F32)
    for head, cols in enumerate(heads):
        grad_scores = scores_buf[head]
        grad_values = dot(probs_ref[head].astype(BF16), mixed_buf[:, cols], TN)
        grad_normed = (
            dot(grad_scores, k_ref[:, cols], NN) * gq_ref[:, cols]
            + dot(grad_scores, q_ref[:, cols], TN) * gk_ref[:, cols]
            + grad_values * gv_ref[:, cols]
        )
        inner = inner + grad_normed * x_ref[:, cols].astype(F32)
        sum_ref[:, cols] = grad_buf[:, cols].astype(F32) + grad_normed * inverse
    inner_ref[...] = jnp.sum(inner, axis=1, keepdims=True)


def finish_kernel(sum_ref, inner_ref, inner_other_ref, x_ref, total_ref, out_ref):
    full = 2 * x_ref.shape[1]
    inverse = lax.rsqrt(total_ref[...] / full + EPS)
    inner = inner_ref[...] + inner_other_ref[...]
    factor = inner * inverse * inverse * inverse / full
    out_ref[...] = (sum_ref[...] - x_ref[...].astype(F32) * factor).astype(BF16)


def order_kernel(place_ref, mixed_ref, held_ref, token_ref, sems):
    token_ref[...] = jnp.zeros_like(token_ref)
    count = sems.shape[0]
    rows = mixed_ref.shape[0] // count
    copies = []
    for i in range(count):
        row = lax.rem(place_ref[0] - i // SIDE + SIDE, SIDE)
        col = lax.rem(place_ref[1] - i % SIDE + SIDE, SIDE)
        source = pl.multiple_of((row * SIDE + col) * rows, rows)
        target = held_ref.at[pl.ds(i * rows, rows)]
        copies.append(
            pltpu.make_async_copy(mixed_ref.at[pl.ds(source, rows)], target, sems.at[i])
        )
    start_all(copies)
    for copy in copies:
        copy.wait()


def weight_kernel(place_ref, *refs):
    columns, (mixed_ref, own_ref, far_ref, total) = refs[: 2 * SIDE], refs[2 * SIDE :]
    plane = place_ref[2]
    shard = own_ref.shape[0]
    size = mixed_ref.shape[0] // SIDE
    here = jnp.full(columns[0].shape[1:], place_ref[0] // 2 == place_ref[3])
    for i in range(SIDE):
        blocks = [jnp.where(here, columns[i][j], columns[SIDE + i][j]) for j in range(SIDE)]
        part = dot(jnp.concatenate(blocks, axis=1), mixed_ref[i * size : (i + 1) * size], NN)
        total[...] = part if i == 0 else total[...] + part
    own_ref[...] = total[pl.ds(pl.multiple_of(plane * shard, 16), shard)]
    far_ref[...] = total[pl.ds(pl.multiple_of((1 - plane) * shard, 16), shard)].astype(BF16)


VMEM = pl.BlockSpec(memory_space=pltpu.VMEM)
SMEM = pl.BlockSpec(memory_space=pltpu.SMEM)
ANY = pl.BlockSpec(memory_space=pl.ANY)


def call(kernel, outs, in_specs, scratch, name, limit, out_specs=None):
    return pl.pallas_call(
        kernel,
        out_shape=tuple(jax.ShapeDtypeStruct(shape, kind) for shape, kind in outs),
        in_specs=in_specs,
        out_specs=out_specs or (VMEM,) * len(outs),
        scratch_shapes=scratch,
        compiler_params=pltpu.CompilerParams(vmem_limit_bytes=limit * MIB),
        name=name,
    )


def local(tokens_in, query_gain, key_gain, value_gain, out_weight, doc_lengths, grad_out):
    rows, width = tokens_in.shape
    full = 2 * width
    heads = width // HEAD_DIM
    shard = out_weight.shape[2]
    sections = lax.axis_size("section")
    section = lax.axis_index("section")
    half = lax.axis_index("tensor")
    index = lax.axis_index("dp")
    plane = index % PLANES
    x_at = index // PLANES % SIDE
    y_at = index // (PLANES * SIDE)
    place = jnp.stack([y_at, x_at, plane, half]).astype(jnp.int32)
    is_first = (section == 0).astype(jnp.int32).reshape(1)
    is_last = (section == sections - 1).astype(jnp.int32).reshape(1)

    ends = jnp.cumsum(doc_lengths[0])
    ident = jnp.sum(
        (jnp.arange(rows, dtype=jnp.int32)[:, None] >= ends[None, :]).astype(jnp.int32), axis=1
    )
    gains = (query_gain, key_gain, value_gain)
    fixed = gains + (ident[:, None], ident[None, :])
    block, column = (rows, width), (rows, 1)
    buffers = [pltpu.VMEM((heads, rows, rows), BF16), pltpu.VMEM(block, BF16)]

    def row_squares(part):
        own = call(squares_kernel, [(column, F32)], [VMEM], [], "row_squares", 8)(part)[0]
        return own, swap(own)

    def summed(base, other):
        shape = [(block, BF16)]
        return call(output_kernel, shape, [VMEM] * 2, [], "layer_output", 8)(base, swap(other))[0]

    first_squares = row_squares(tokens_in)
    (mixed,) = call(
        attention_kernel, [(block, BF16)], [VMEM] * 8, buffers, "first_attention", 12
    )(tokens_in, *first_squares, *fixed)
    pieces = gather_weight(out_weight[0].T)
    layout = tuple(piece[:3] for piece in pieces)
    base, other, weight_rows = call(
        lambda *refs: first_kernel(layout, *refs),
        [(block, F32), (block, BF16), ((full, width), BF16)],
        [SMEM, VMEM, VMEM] + [ANY] * len(layout),
        [
            pltpu.VMEM((full, width), BF16),
            pltpu.VMEM((rows, full), BF16),
            pltpu.SemaphoreType.DMA((SIDE, len(layout))),
            pltpu.SemaphoreType.DMA((SIDE,)),
        ],
        "first_forward",
        58,
        (VMEM, VMEM, ANY),
    )(place, tokens_in, mixed, *[piece[3] for piece in pieces])
    output = summed(base, other)
    (weight_rows,) = tied([weight_rows], output)
    token = ((8, HEAD_DIM), F32)
    weight_cols, turned = call(
        turn_kernel, [((width, full), BF16), token], [VMEM], [], "turn_weight", 28
    )(weight_rows)

    forward = call(
        forward_kernel,
        [(block, F32), (block, BF16), (block, BF16), (block, BF16), (column, F32)],
        [SMEM] + [VMEM] * 13,
        buffers,
        "layer_forward",
        20,
    )
    for turn in range(1, sections):
        arrived = relay(output, 1)
        if turn == 1:
            arrived, ready = lax.optimization_barrier((arrived, turned))
        base, other, mixed, x, squares = forward(
            is_first, tokens_in, *first_squares, arrived, *row_squares(arrived), *fixed, ready, weight_cols
        )
        output = summed(base, other)

    planes = [
        [grid_index(y, x, p) for y in range(SIDE) for x in range(SIDE)] for p in range(PLANES)
    ]
    mixed_all = lax.all_gather(mixed, "dp", axis_index_groups=planes, axis=0, tiled=True)
    probs, queries, keys, values = call(
        prepare_kernel,
        [((heads, rows, rows), F32), (block, BF16), (block, BF16), (block, BF16)],
        [VMEM] * 7,
        [],
        "backward_probs",
        12,
    )(x, squares, *fixed)
    backward = call(
        backward_kernel,
        [(block, F32), (column, F32)],
        [SMEM] + [VMEM] * 14,
        [
            pltpu.VMEM((rows, full), BF16),
            pltpu.VMEM(block, BF16),
            pltpu.VMEM((heads, rows, rows), BF16),
        ],
        "layer_backward",
        22,
    )
    finish = call(finish_kernel, [(block, BF16)], [VMEM] * 5, [], "input_gradient", 8)
    given = (grad_out, swap(grad_out))

    def input_gradient(arrived, held):
        pulled, inner = backward(
            is_last, *given, *arrived, x, squares, *gains, probs, queries, keys, values, held
        )
        return finish(pulled, inner, swap(inner), x, squares)[0]

    def passed(grad_in):
        grad = relay(grad_in, -1)
        return grad, swap(grad)

    grad_in = input_gradient(given, weight_rows)
    for turn in range(1, sections - 1):
        grad_in = input_gradient(passed(grad_in), weight_rows)
    arrived = passed(grad_in)

    columns, ordered = exchange_columns(place, is_last, grad_out, arrived[0], mixed_all)
    near, far = call(
        weight_kernel,
        [((shard, width), F32), ((shard, width), BF16)],
        [SMEM] + [VMEM] * (2 * SIDE + 1),
        [pltpu.VMEM((PLANES * shard, width), F32)],
        "weight_gradient",
        24,
    )(place, *columns, ordered)
    far_sum = shift(far, "plane", 1)
    grad_in = input_gradient(tied(arrived, far), weight_rows)
    weight_grads = (near + far_sum.astype(F32)).T
    return output[None], grad_in[None], weight_grads[None]


def solution(mesh):
    return jax.shard_map(
        local,
        mesh=mesh,
        in_specs=(
            P("dp", "tensor"),
            P("section", "tensor"),
            P("section", "tensor"),
            P("section", "tensor"),
            P("section", "tensor", "dp"),
            P("dp", None),
            P("dp", "tensor"),
        ),
        out_specs=(
            P("section", "dp", "tensor"),
            P("section", "dp", "tensor"),
            P("section", "tensor", "dp"),
        ),
        check_vma=False,
    )
```

```python
import jax
import jax.numpy as jnp
from jax import lax
from jax.experimental import pallas as pl
from jax.experimental.pallas import tpu as pltpu
from jax.sharding import PartitionSpec as P

HEAD_DIM = 128
EPS = 1e-05
CHUNK = 256
SIDE = 4
PLANES = 2
F32 = jnp.float32
BF16 = jnp.bfloat16
NN = (((1,), (0,)), ((), ()))
NT = (((1,), (1,)), ((), ()))
TN = (((0,), (0,)), ((), ()))
MIB = 1024 * 1024
FIRST_OFFSETS = (0, -1, -2, 1)


def dot(a, b, dims):
    return lax.dot_general(a, b, dims, preferred_element_type=F32)


def split(a):
    high = a.astype(BF16)
    return high, (a - high.astype(F32)).astype(BF16)


def grid_index(y, x, plane):
    return ((y % SIDE) * SIDE + x % SIDE) * PLANES + plane % PLANES


def shift(block, axis, step):
    move = {"y": (step, 0, 0), "x": (0, step, 0), "plane": (0, 0, step)}[axis]
    route = [
        (grid_index(y, x, p), grid_index(y + move[0], x + move[1], p + move[2]))
        for y in range(SIDE)
        for x in range(SIDE)
        for p in range(PLANES)
    ]
    return lax.ppermute(block, "dp", route)


def tied(blocks, *others):
    return list(lax.optimization_barrier(tuple(blocks) + tuple(others))[: len(blocks)])


def gather_weight(shard):
    width = shard.shape[1] // 2
    sides = ((slice(0, width), "x", "y"), (slice(width, 2 * width), "y", "x"))
    seconds = [side[2] for side in sides]

    def first_ring(block):
        joined = []
        for cols, axis, _ in sides:
            own = block[:, cols]
            back, ahead = shift(own, axis, 1), shift(own, axis, -1)
            joined.append(jnp.concatenate([own, back, shift(back, axis, 1), ahead], axis=0))
        return joined

    def both(blocks, step):
        return [shift(block, axis, step) for block, axis in zip(blocks, seconds)]

    far_shard = shift(shard, "plane", 1)
    near = tied(first_ring(shard))
    near_back, near_ahead = both(near, 1), both(near, -1)
    far_shard, *moved = lax.optimization_barrier((far_shard, *near_back, *near_ahead))
    near_back, near_ahead = moved[:2], moved[2:]
    near_across = both(near_back, 1)
    far = tied(first_ring(far_shard))
    far_ahead = both(far, -1)
    late = tied(far, *near_across)
    far_back = both(late, 1)
    far_across = both(far_ahead, -1)
    pieces = []
    for side in range(2):
        for plane, group in enumerate(
            ((near, near_back, near_ahead, near_across), (far, far_back, far_ahead, far_across))
        ):
            for offset, blocks in zip((0, -1, 1, -2), group):
                pieces.append((side, plane, offset, blocks[side]))
    return pieces


def exchange_columns(place, is_last, given, arrived, mixed_all):
    rows, width = given.shape
    size = width // (2 * SIDE)
    chunks = call(
        columns_kernel,
        [((2, size, rows), BF16)] * SIDE,
        [SMEM, SMEM, VMEM, VMEM],
        [pltpu.VMEM((width, rows), BF16)],
        "cut_columns",
        12,
    )(place, is_last, given, arrived)
    ordered, token = call(
        order_kernel,
        [(mixed_all.shape, BF16), ((8, HEAD_DIM), F32)],
        [SMEM, ANY],
        [pltpu.SemaphoreType.DMA((SIDE * SIDE,))],
        "order_mixed",
        40,
    )(place, tied([mixed_all], *chunks)[0])
    parts = [shift(chunk, "x", step) if step else chunk for step, chunk in enumerate(chunks)]
    *parts, token = lax.optimization_barrier((*parts, token))
    parts = call(
        pick_kernel,
        [((SIDE, size, rows), BF16)] * SIDE,
        [SMEM] + [VMEM] * (SIDE + 1),
        [],
        "pick_columns",
        12,
    )(place, token, *parts)
    result = []
    for step, part in enumerate(parts):
        if step:
            route = []
            for row in range(SIDE):
                target = (row + step) % SIDE
                for col in range(SIDE):
                    for p in range(PLANES):
                        source, sink = grid_index(row, col, p), grid_index(target, col, p)
                        route.append((source * 2 + target // 2, sink * 2 + target // 2))
            part = lax.ppermute(part, ("dp", "tensor"), route)
        result.append(part)
    return result + [swap(part) for part in result], ordered


def swap(block):
    return lax.ppermute(block, "tensor", [(0, 1), (1, 0)])


def relay(block, step):
    sections = lax.axis_size("section")
    route = [(i, i + step) for i in range(sections) if 0 <= i + step < sections]
    return lax.ppermute(block, "section", route)


def allowed_mask(id_col, id_row):
    shape = (id_col.shape[0], id_row.shape[1])
    rows = lax.broadcasted_iota(jnp.int32, shape, 0)
    cols = lax.broadcasted_iota(jnp.int32, shape, 1)
    return (rows >= cols) & (id_col[...] == id_row[...])


def softmax(scores, allowed):
    scores = jnp.where(allowed, scores * HEAD_DIM**-0.5, -1e30)
    expo = jnp.exp(scores - jnp.max(scores, axis=1, keepdims=True))
    return expo / jnp.sum(expo, axis=1, keepdims=True)


def head_slices(width):
    return [slice(i, i + HEAD_DIM) for i in range(0, width, HEAD_DIM)]


def attend(x_ref, inverse, gq_ref, gk_ref, gv_ref, id_col, id_row, probs_buf, values_buf, mixed_ref):
    allowed = allowed_mask(id_col, id_row)
    heads = head_slices(x_ref.shape[1])
    for head, cols in enumerate(heads):
        normed = x_ref[:, cols].astype(F32) * inverse
        queries = (normed * gq_ref[:, cols]).astype(BF16)
        keys = (normed * gk_ref[:, cols]).astype(BF16)
        values_buf[:, cols] = (normed * gv_ref[:, cols]).astype(BF16)
        probs_buf[head] = softmax(dot(queries, keys, NT), allowed).astype(BF16)
    for head, cols in enumerate(heads):
        mixed_ref[:, cols] = dot(probs_buf[head], values_buf[:, cols], NN).astype(BF16)


def inverse_norm(squares_ref, squares_other_ref, full):
    return lax.rsqrt((squares_ref[...] + squares_other_ref[...]) / full + EPS)


def start_all(copies):
    for copy in copies:
        copy.start()


def attention_kernel(x_ref, squares_ref, squares_other_ref, *refs):
    inverse = inverse_norm(squares_ref, squares_other_ref, 2 * x_ref.shape[1])
    fixed, (mixed_ref, probs_buf, values_buf) = refs[:5], refs[5:]
    attend(x_ref, inverse, *fixed, probs_buf, values_buf, mixed_ref)


def first_kernel(layout, place_ref, x_ref, mixed_ref, *refs):
    pieces, refs = refs[: len(layout)], refs[len(layout) :]
    base_ref, other_ref, rows_out, held, product, sems, out_sems = refs
    y, x, plane, half = [place_ref[i] for i in range(4)]
    full, width = held.shape
    shard = pieces[0].shape[0] // SIDE
    groups = [[] for _ in range(SIDE)]
    for (side, far, offset), piece in zip(layout, pieces):
        for part, first in enumerate(FIRST_OFFSETS):
            at_y, at_x = (offset, first) if side == 0 else (first, offset)
            row = lax.rem(y + at_y + SIDE, SIDE)
            col = lax.rem(x + at_x + SIDE, SIDE)
            depth = 1 - plane if far else plane
            start = lax.rem(((row * SIDE + col) * PLANES + depth) * shard + half * width, full)
            start = pl.multiple_of(start, 16)
            group = groups[-at_y % SIDE]
            group.append(
                pltpu.make_async_copy(
                    piece.at[pl.ds(part * shard, shard)],
                    held.at[pl.ds(start, shard), pl.ds(side * (width // 2), width // 2)],
                    sems.at[-at_y % SIDE, len(group)],
                )
            )
    for group in groups:
        start_all(group)
    mixed = mixed_ref[...]
    block = full // SIDE
    outs = []
    for step, group in enumerate(groups):
        for copy in group:
            copy.wait()
        start = lax.rem(lax.rem(y - step + SIDE, SIDE) * block + half * width, full)
        start = pl.multiple_of(start, HEAD_DIM)
        rows = pl.ds(start, block)
        outs.append(pltpu.make_async_copy(held.at[rows], rows_out.at[rows], out_sems.at[step]))
        outs[-1].start()
        for i in range(0, block, CHUNK):
            at = pl.multiple_of(start + i, HEAD_DIM)
            size = min(CHUNK, block - i)
            part = dot(mixed, held[pl.ds(at, size), :], NT)
            product[:, pl.ds(at, size)] = part.astype(BF16)
    base_ref[...] = x_ref[...].astype(F32) + product[:, :width].astype(F32)
    other_ref[...] = product[:, width:]
    for out in outs:
        out.wait()


def turn_kernel(rows_ref, cols_ref, token_ref):
    token_ref[...] = jnp.zeros_like(token_ref)
    for i in range(0, rows_ref.shape[0], CHUNK):
        cols_ref[:, i : i + CHUNK] = rows_ref[i : i + CHUNK, :].T


def output_kernel(base_ref, other_ref, out_ref):
    out_ref[...] = (base_ref[...] + other_ref[...].astype(F32)).astype(BF16)


def squares_kernel(x_ref, out_ref):
    total = jnp.zeros((x_ref.shape[0], HEAD_DIM), F32)
    for cols in head_slices(x_ref.shape[1]):
        part = x_ref[:, cols].astype(F32)
        total = total + part * part
    out_ref[...] = jnp.sum(total, axis=1, keepdims=True)


def columns_kernel(place_ref, is_last, given_ref, arrived_ref, *refs):
    outs, turned = refs[:-1], refs[-1]

    @pl.when(is_last[0] == 1)
    def _():
        turned[...] = given_ref[...].T

    @pl.when(is_last[0] == 0)
    def _():
        turned[...] = arrived_ref[...].T

    size = outs[0].shape[1]
    for step, out in enumerate(outs):
        col = lax.rem(place_ref[1] + step, SIDE)
        for i in range(2):
            start = pl.multiple_of((i * SIDE + col) * size, 16)
            out[i] = turned[pl.ds(start, size), :]


def pick_kernel(place_ref, token_ref, *refs):
    parts, outs = refs[:SIDE], refs[SIDE:]
    for step, out in enumerate(outs):
        which = lax.rem(place_ref[0] + step, 2)
        for i, part in enumerate(parts):
            out[i] = part[which]


def forward_kernel(
    is_first, tokens_ref, tokens_squares, tokens_squares_other, arrived_ref, squares_ref,
    squares_other_ref, *refs,
):
    fixed, refs = refs[:5], refs[6:]
    cols_ref, base_ref, other_ref, mixed_ref, x_ref, total_ref, probs_buf, values_buf = refs

    @pl.when(is_first[0] == 1)
    def _():
        x_ref[...] = tokens_ref[...]
        total_ref[...] = tokens_squares[...] + tokens_squares_other[...]

    @pl.when(is_first[0] == 0)
    def _():
        x_ref[...] = arrived_ref[...]
        total_ref[...] = squares_ref[...] + squares_other_ref[...]

    width = x_ref.shape[1]
    inverse = lax.rsqrt(total_ref[...] / (2 * width) + EPS)
    attend(x_ref, inverse, *fixed, probs_buf, values_buf, mixed_ref)
    mixed = mixed_ref[...]
    for i in range(0, width, CHUNK):
        cols = slice(i, i + CHUNK)
        own = dot(mixed, cols_ref[:, cols], NN).astype(BF16)
        base_ref[:, cols] = x_ref[:, cols].astype(F32) + own.astype(F32)
        other_ref[:, cols] = dot(mixed, cols_ref[:, width + i : width + i + CHUNK], NN).astype(BF16)


def prepare_kernel(
    x_ref, total_ref, gq_ref, gk_ref, gv_ref, id_col, id_row, probs_ref, q_ref, k_ref, v_ref
):
    width = x_ref.shape[1]
    inverse = lax.rsqrt(total_ref[...] / (2 * width) + EPS)
    allowed = allowed_mask(id_col, id_row)
    for head, cols in enumerate(head_slices(width)):
        normed = x_ref[:, cols].astype(F32) * inverse
        q_high, q_low = split(normed * gq_ref[:, cols])
        k_high, k_low = split(normed * gk_ref[:, cols])
        q_ref[:, cols] = q_high
        k_ref[:, cols] = k_high
        v_ref[:, cols] = (normed * gv_ref[:, cols]).astype(BF16)
        scores = dot(
            jnp.concatenate([q_high, q_high, q_low], axis=1),
            jnp.concatenate([k_high, k_low, k_high], axis=1),
            NT,
        )
        probs_ref[head] = softmax(scores, allowed)


def backward_kernel(
    is_last, given_ref, given_other_ref, arrived_ref, arrived_other_ref, x_ref, total_ref, gq_ref,
    gk_ref, gv_ref, probs_ref, q_ref, k_ref, v_ref, rows_ref, sum_ref, inner_ref, grad_buf,
    mixed_buf, scores_buf,
):
    full, width = rows_ref.shape

    @pl.when(is_last[0] == 1)
    def _():
        grad_buf[:, :width] = given_ref[...]
        grad_buf[:, width:] = given_other_ref[...]

    @pl.when(is_last[0] == 0)
    def _():
        grad_buf[:, :width] = arrived_ref[...]
        grad_buf[:, width:] = arrived_other_ref[...]

    inverse = lax.rsqrt(total_ref[...] / full + EPS)
    heads = head_slices(width)
    for i in range(0, width, CHUNK):
        cols = slice(i, i + CHUNK)
        mixed_buf[:, cols] = dot(grad_buf[...], rows_ref[:, cols], NN).astype(BF16)
    for head, cols in enumerate(heads):
        probs = probs_ref[head]
        weighted = probs * dot(mixed_buf[:, cols], v_ref[:, cols], NT)
        inner = jnp.sum(weighted, axis=1, keepdims=True)
        scores_buf[head] = ((weighted - probs * inner) * HEAD_DIM**-0.5).astype(BF16)
    inner = jnp.zeros((x_ref.shape[0], HEAD_DIM), F32)
    for head, cols in enumerate(heads):
        grad_scores = scores_buf[head]
        grad_values = dot(probs_ref[head].astype(BF16), mixed_buf[:, cols], TN)
        grad_normed = (
            dot(grad_scores, k_ref[:, cols], NN) * gq_ref[:, cols]
            + dot(grad_scores, q_ref[:, cols], TN) * gk_ref[:, cols]
            + grad_values * gv_ref[:, cols]
        )
        inner = inner + grad_normed * x_ref[:, cols].astype(F32)
        sum_ref[:, cols] = grad_buf[:, cols].astype(F32) + grad_normed * inverse
    inner_ref[...] = jnp.sum(inner, axis=1, keepdims=True)


def finish_kernel(sum_ref, inner_ref, inner_other_ref, x_ref, total_ref, out_ref):
    full = 2 * x_ref.shape[1]
    inverse = lax.rsqrt(total_ref[...] / full + EPS)
    inner = inner_ref[...] + inner_other_ref[...]
    factor = inner * inverse * inverse * inverse / full
    out_ref[...] = (sum_ref[...] - x_ref[...].astype(F32) * factor).astype(BF16)


def order_kernel(place_ref, mixed_ref, held_ref, token_ref, sems):
    token_ref[...] = jnp.zeros_like(token_ref)
    count = sems.shape[0]
    rows = mixed_ref.shape[0] // count
    copies = []
    for i in range(count):
        row = lax.rem(place_ref[0] - i // SIDE + SIDE, SIDE)
        col = lax.rem(place_ref[1] - i % SIDE + SIDE, SIDE)
        source = pl.multiple_of((row * SIDE + col) * rows, rows)
        target = held_ref.at[pl.ds(i * rows, rows)]
        copies.append(
            pltpu.make_async_copy(mixed_ref.at[pl.ds(source, rows)], target, sems.at[i])
        )
    start_all(copies)
    for copy in copies:
        copy.wait()


def weight_kernel(place_ref, *refs):
    columns, (mixed_ref, own_ref, far_ref, total) = refs[: 2 * SIDE], refs[2 * SIDE :]
    plane = place_ref[2]
    shard = own_ref.shape[0]
    size = mixed_ref.shape[0] // SIDE
    here = jnp.full(columns[0].shape[1:], place_ref[0] // 2 == place_ref[3])
    for i in range(SIDE):
        blocks = [jnp.where(here, columns[i][j], columns[SIDE + i][j]) for j in range(SIDE)]
        part = dot(jnp.concatenate(blocks, axis=1), mixed_ref[i * size : (i + 1) * size], NN)
        total[...] = part if i == 0 else total[...] + part
    own_ref[...] = total[pl.ds(pl.multiple_of(plane * shard, 16), shard)]
    far_ref[...] = total[pl.ds(pl.multiple_of((1 - plane) * shard, 16), shard)].astype(BF16)


VMEM = pl.BlockSpec(memory_space=pltpu.VMEM)
SMEM = pl.BlockSpec(memory_space=pltpu.SMEM)
ANY = pl.BlockSpec(memory_space=pl.ANY)


def call(kernel, outs, in_specs, scratch, name, limit, out_specs=None):
    return pl.pallas_call(
        kernel,
        out_shape=tuple(jax.ShapeDtypeStruct(shape, kind) for shape, kind in outs),
        in_specs=in_specs,
        out_specs=out_specs or (VMEM,) * len(outs),
        scratch_shapes=scratch,
        compiler_params=pltpu.CompilerParams(vmem_limit_bytes=limit * MIB),
        name=name,
    )


def local(tokens_in, query_gain, key_gain, value_gain, out_weight, doc_lengths, grad_out):
    rows, width = tokens_in.shape
    full = 2 * width
    heads = width // HEAD_DIM
    shard = out_weight.shape[2]
    sections = lax.axis_size("section")
    section = lax.axis_index("section")
    half = lax.axis_index("tensor")
    index = lax.axis_index("dp")
    plane = index % PLANES
    x_at = index // PLANES % SIDE
    y_at = index // (PLANES * SIDE)
    place = jnp.stack([y_at, x_at, plane, half]).astype(jnp.int32)
    is_first = (section == 0).astype(jnp.int32).reshape(1)
    is_last = (section == sections - 1).astype(jnp.int32).reshape(1)

    ends = jnp.cumsum(doc_lengths[0])
    ident = jnp.sum(
        (jnp.arange(rows, dtype=jnp.int32)[:, None] >= ends[None, :]).astype(jnp.int32), axis=1
    )
    gains = (query_gain, key_gain, value_gain)
    fixed = gains + (ident[:, None], ident[None, :])
    block, column = (rows, width), (rows, 1)
    buffers = [pltpu.VMEM((heads, rows, rows), BF16), pltpu.VMEM(block, BF16)]

    def row_squares(part):
        own = call(squares_kernel, [(column, F32)], [VMEM], [], "row_squares", 8)(part)[0]
        return own, swap(own)

    def summed(base, other):
        shape = [(block, BF16)]
        return call(output_kernel, shape, [VMEM] * 2, [], "layer_output", 8)(base, swap(other))[0]

    first_squares = row_squares(tokens_in)
    (mixed,) = call(
        attention_kernel, [(block, BF16)], [VMEM] * 8, buffers, "first_attention", 12
    )(tokens_in, *first_squares, *fixed)
    pieces = gather_weight(out_weight[0].T)
    layout = tuple(piece[:3] for piece in pieces)
    base, other, weight_rows = call(
        lambda *refs: first_kernel(layout, *refs),
        [(block, F32), (block, BF16), ((full, width), BF16)],
        [SMEM, VMEM, VMEM] + [ANY] * len(layout),
        [
            pltpu.VMEM((full, width), BF16),
            pltpu.VMEM((rows, full), BF16),
            pltpu.SemaphoreType.DMA((SIDE, len(layout))),
            pltpu.SemaphoreType.DMA((SIDE,)),
        ],
        "first_forward",
        58,
        (VMEM, VMEM, ANY),
    )(place, tokens_in, mixed, *[piece[3] for piece in pieces])
    output = summed(base, other)
    (weight_rows,) = tied([weight_rows], output)
    token = ((8, HEAD_DIM), F32)
    weight_cols, turned = call(
        turn_kernel, [((width, full), BF16), token], [VMEM], [], "turn_weight", 28
    )(weight_rows)

    summands = [(block, F32), (block, BF16)]
    saved = [(block, BF16), (block, BF16), (column, F32)]
    inputs = [SMEM] + [VMEM] * 13
    unsaved = [pltpu.VMEM(*part) for part in saved]
    forward = call(forward_kernel, summands, inputs, unsaved + buffers, "layer_forward", 20)
    last_forward = call(forward_kernel, summands + saved, inputs, buffers, "last_forward", 20)
    for turn in range(1, sections):
        arrived = relay(output, 1)
        if turn == 1:
            arrived, ready = lax.optimization_barrier((arrived, turned))
        layer = last_forward if turn == sections - 1 else forward
        base, other, *kept = layer(
            is_first, tokens_in, *first_squares, arrived, *row_squares(arrived), *fixed, ready, weight_cols
        )
        output = summed(base, other)

    mixed, x, squares = kept
    planes = [
        [grid_index(y, x, p) for y in range(SIDE) for x in range(SIDE)] for p in range(PLANES)
    ]
    mixed_all = lax.all_gather(mixed, "dp", axis_index_groups=planes, axis=0, tiled=True)
    probs, queries, keys, values = call(
        prepare_kernel,
        [((heads, rows, rows), F32), (block, BF16), (block, BF16), (block, BF16)],
        [VMEM] * 7,
        [],
        "backward_probs",
        12,
    )(x, squares, *fixed)
    backward = call(
        backward_kernel,
        [(block, F32), (column, F32)],
        [SMEM] + [VMEM] * 14,
        [
            pltpu.VMEM((rows, full), BF16),
            pltpu.VMEM(block, BF16),
            pltpu.VMEM((heads, rows, rows), BF16),
        ],
        "layer_backward",
        22,
    )
    finish = call(finish_kernel, [(block, BF16)], [VMEM] * 5, [], "input_gradient", 8)
    given = (grad_out, swap(grad_out))

    def input_gradient(arrived, held):
        pulled, inner = backward(
            is_last, *given, *arrived, x, squares, *gains, probs, queries, keys, values, held
        )
        return finish(pulled, inner, swap(inner), x, squares)[0]

    def passed(grad_in):
        grad = relay(grad_in, -1)
        return grad, swap(grad)

    grad_in = input_gradient(given, weight_rows)
    for turn in range(1, sections - 1):
        grad_in = input_gradient(passed(grad_in), weight_rows)
    arrived = passed(grad_in)

    columns, ordered = exchange_columns(place, is_last, grad_out, arrived[0], mixed_all)
    near, far = call(
        weight_kernel,
        [((shard, width), F32), ((shard, width), BF16)],
        [SMEM] + [VMEM] * (2 * SIDE + 1),
        [pltpu.VMEM((PLANES * shard, width), F32)],
        "weight_gradient",
        24,
    )(place, *columns, ordered)
    far_sum = shift(far, "plane", 1)
    grad_in = input_gradient(tied(arrived, far), weight_rows)
    weight_grads = (near + far_sum.astype(F32)).T
    return output[None], grad_in[None], weight_grads[None]


def solution(mesh):
    return jax.shard_map(
        local,
        mesh=mesh,
        in_specs=(
            P("dp", "tensor"),
            P("section", "tensor"),
            P("section", "tensor"),
            P("section", "tensor"),
            P("section", "tensor", "dp"),
            P("dp", None),
            P("dp", "tensor"),
        ),
        out_specs=(
            P("section", "dp", "tensor"),
            P("section", "dp", "tensor"),
            P("section", "tensor", "dp"),
        ),
        check_vma=False,
    )
```
